768 devices in a mesh: gz: 96 (over x, z, core), gy: 8 (over y).
Axes of the slice: x: 4, y: 8, z: 12, core: 2. Of those that a mesh axis runs over, the one named last changes fastest.
Arguments:
- source: float32 [384, 128, 512], P('gz', 'gy'), may hold values from -8 to 8
- conduct: float32 [384, 128, 512], P('gz', 'gy'), may hold values from 0.5 to 4
Outputs:
- adjoint: float32 [384, 128, 512], P('gz', 'gy')
- residual: float32 [384, 128, 512], P('gz', 'gy')
The draws below stay inside these ranges and needn't reach their ends.
All inputs are finite; a program needn't handle non-finite values.
Results may differ from the reference program's by a relative error of at most 0.0003.
Values sent between devices are 32-bit elements; how exact they have to be, the bound alone decides.
No kernel may reach another device: no remote copies, remote signals or barrier semaphores. Data moves between devices by JAX's collectives and lax.ppermute only.
A program may use at most 64 MiB of HBM per device.

```python
import math
import jax
import jax.numpy as jnp

NX = 512
DEGREE = 3
COARSE_DEGREE = 4
CYCLES = 2
NZ = 384
NY = 128


def levels(stream_key, dims, split, least, largest):
    gain, own = 1.0, jax.random.fold_in(stream_key, 6)
    for axis_at, shards_of in split:
        heights = jnp.exp(jax.random.uniform(jax.random.fold_in(own, axis_at), (shards_of,), jnp.float32, least / len(split), largest / len(split)))
        gain = gain * jnp.repeat(heights, dims[axis_at] // shards_of).reshape([-1 if axis == axis_at else 1 for axis in range(len(dims))])
    return gain


def normal_values(stream_key, extent, deviation, most, cuts=(), kind=jnp.bfloat16):
    factor_of = levels(stream_key, extent, cuts, -0.22, 0.18) if cuts else 1.0
    entries = jax.random.normal(stream_key, extent, jnp.float32) * deviation * factor_of
    return jnp.minimum(jnp.maximum(entries, -most), most).astype(kind)


def setup_inputs(seed: int = 0) -> dict:
    splits = jax.random.split(jax.random.key(seed), 3)
    source = normal_values(splits[0], (NZ, NY, NX), 1.0, 8.0, ((0, 96), (1, 8)), jnp.float32)
    conduct = jnp.clip(jnp.exp(math.log(4.0) - 2.0794415 * jax.random.uniform(splits[1], (NZ, NY, NX), jnp.float32) ** levels(splits[1], (NZ, NY, NX), ((0, 96), (1, 8)), -0.2, 0.2)), 0.5, 4.0)
    return {"source": source, "conduct": conduct}


cheb_low = 0.3
cheb_high = 1.9
heat_step = 4.0


def apply_level(field, conduct, scale):
    w = conduct * field
    beside = jnp.roll(w, -1, 0) + jnp.roll(w, 1, 0)
    beside = beside + jnp.roll(w, -1, 1) + jnp.roll(w, 1, 1)
    padded = jnp.pad(w, ((0, 0), (0, 0), (1, 1)))
    beside = beside + padded[:, :, 2:] + padded[:, :, :-2]
    return field + scale * (6.0 * w - beside)


def restrict(field):
    z, y, x = field.shape
    return field.reshape(z // 2, 2, y // 2, 2, x // 2, 2).mean(axis=(1, 3, 5))


def prolong(field):
    return jnp.repeat(jnp.repeat(jnp.repeat(field, 2, 0), 2, 1), 2, 2)


def smooth(apply_fn, rhs, start, inv_diag, steps):
    theta = (cheb_high + cheb_low) / 2.0
    delta = (cheb_high - cheb_low) / 2.0
    sigma = theta / delta
    rho = 1.0 / sigma
    if start is None:
        correct = inv_diag * rhs
        change = correct / theta
        field = change
    else:
        correct = inv_diag * (rhs - apply_fn(start))
        change = correct / theta
        field = start + change
    for step in range(steps - 1):
        rho_next = 1.0 / (2.0 * sigma - rho)
        correct = inv_diag * (rhs - apply_fn(field))
        change = rho_next * rho * change + (2.0 * rho_next / delta) * correct
        field = field + change
        rho = rho_next
    return field


def vcycle(rhs, conducts, scales):
    ops = [partial_apply(conducts[i], scales[i]) for i in range(3)]
    diags = [1.0 / (1.0 + 6.0 * scales[i] * conducts[i]) for i in range(3)]
    fine = smooth(ops[0], rhs, None, diags[0], DEGREE)
    rhs_mid = restrict(rhs - ops[0](fine))
    middle = smooth(ops[1], rhs_mid, None, diags[1], DEGREE)
    rhs_low = restrict(rhs_mid - ops[1](middle))
    lowest = smooth(ops[2], rhs_low, None, diags[2], COARSE_DEGREE)
    middle = smooth(ops[1], rhs_mid, middle + prolong(lowest), diags[1], DEGREE)
    fine = smooth(ops[0], rhs, fine + prolong(middle), diags[0], DEGREE)
    return fine


def partial_apply(conduct, scale):
    def inner(field):
        return apply_level(field, conduct, scale)
    return inner


def reference(source, conduct):
    mid_cond = restrict(conduct)
    conducts = [conduct, mid_cond, restrict(mid_cond)]
    scales = [heat_step, heat_step / 4.0, heat_step / 16.0]
    adjoint = jnp.zeros_like(source)
    remain = source
    for cycle in range(CYCLES):
        adjoint = adjoint + vcycle(remain, conducts, scales)
        remain = source - apply_level(adjoint, conduct, heat_step)
    return adjoint, remain
```

```python
import functools

import jax
import jax.numpy as jnp
from jax import lax
from jax.experimental import pallas as pl
from jax.experimental.pallas import tpu as pltpu
from jax.sharding import PartitionSpec as P

DEGREE = 3
COARSE_DEGREE = 4
CYCLES = 2

CHEB_LOW = 0.3
CHEB_HIGH = 1.9
SCALES = (4.0, 1.0, 0.25)
LANES = 128
VMEM_LIMIT = 48 * 1024 * 1024


def chebyshev(steps):
    theta = (CHEB_HIGH + CHEB_LOW) / 2.0
    delta = (CHEB_HIGH - CHEB_LOW) / 2.0
    sigma = theta / delta
    rho = 1.0 / sigma
    pairs = [(0.0, 1.0 / theta)]
    for _ in range(steps - 1):
        rho_next = 1.0 / (2.0 * sigma - rho)
        pairs.append((rho_next * rho, 2.0 * rho_next / delta))
        rho = rho_next
    return pairs


def lanes(c):
    return slice(c * LANES, (c + 1) * LANES)


def load(ref, z, size):
    return [[ref[z, d, :, lanes(c)] for c in range(size)] for d in range(size)]


def load_ends(ref, z, size):
    top = ref.shape[2]
    return [
        [
            jnp.concatenate([ref[z, d, 0:8, lanes(c)], ref[z, d, top - 8 : top, lanes(c)]], axis=0)
            for c in range(size)
        ]
        for d in range(size)
    ]


def neighbours(below, here, above, size):
    rows = here[0][0].shape[0]
    lane = lax.broadcasted_iota(jnp.int32, (rows, LANES), 1)
    first, last = lane == 0, lane == LANES - 1
    out = []
    for d in range(size):
        line = []
        for c in range(size):
            if c > 0:
                left = here[d][c - 1]
            else:
                left = jnp.where(first, 0.0, pltpu.roll(here[d][size - 1], 1, 1))
            if c < size - 1:
                right = here[d][c + 1]
            else:
                right = jnp.where(last, 0.0, pltpu.roll(here[d][0], LANES - 1, 1))
            low = here[d - 1][c] if d > 0 else pltpu.roll(here[size - 1][c], 1, 0)
            high = here[d + 1][c] if d < size - 1 else pltpu.roll(here[0][c], rows - 1, 0)
            line.append(((below[d][c] + above[d][c]) + (left + right)) + (low + high))
        out.append(line)
    return out


def first_step(lo, hi, rhs, inv, w, dw, size, beta):
    def body(z, carry):
        for d in range(size):
            for c in range(size):
                value = (beta * rhs[z, d, :, lanes(c)]) * inv[z, d, :, lanes(c)]
                w[z, d, :, lanes(c)] = value
                dw[z, d, :, lanes(c)] = value
        return carry

    lax.fori_loop(lo, hi, body, 0)


def sweep(lo, hi, src, dst, dst_shift, dw, rhs, inv, shift, size, scale, alpha, beta, loader=load):
    def body(z, carry):
        here = load(src, z, size)
        near = neighbours(load(src, z - 1, size), here, load(src, z + 1, size), size)
        f = loader(rhs, z + shift, size)
        i = loader(inv, z + shift, size)
        for d in range(size):
            for c in range(size):
                q = i[d][c] * (f[d][c] + scale * near[d][c]) - here[d][c]
                change = beta * q
                if alpha != 0.0:
                    change = change + alpha * dw[z, d, :, lanes(c)]
                dw[z, d, :, lanes(c)] = change
                dst[z + dst_shift, d, :, lanes(c)] = here[d][c] + change
        return carry

    lax.fori_loop(lo, hi, body, 0)


def residual_plane(src, z, rhs, inv, zr, size, scale):
    here = load(src, z, size)
    near = neighbours(load(src, z - 1, size), here, load(src, z + 1, size), size)
    out = []
    for d in range(size):
        line = []
        for c in range(size):
            i = inv[zr, d, :, lanes(c)]
            line.append((rhs[zr, d, :, lanes(c)] + scale * near[d][c]) - here[d][c] / i)
        out.append(line)
    return out


def halve(one, two, size):
    half = size // 2
    return [
        [
            0.125
            * (
                ((one[2 * d][2 * c] + one[2 * d][2 * c + 1]) + (one[2 * d + 1][2 * c] + one[2 * d + 1][2 * c + 1]))
                + ((two[2 * d][2 * c] + two[2 * d][2 * c + 1]) + (two[2 * d + 1][2 * c] + two[2 * d + 1][2 * c + 1]))
            )
            for c in range(half)
        ]
        for d in range(half)
    ]


def inverse_of(cond, scale):
    return 1.0 / (1.0 / cond + 6.0 * scale)


def selector(to_tiles):
    rows = lax.broadcasted_iota(jnp.int32, (512, 512), 0)
    cols = lax.broadcasted_iota(jnp.int32, (512, 512), 1)
    if to_tiles:
        hit = rows == 4 * (cols % LANES) + cols // LANES
    else:
        hit = cols == 4 * (rows % LANES) + rows // LANES
    return jnp.where(hit, 1.0, 0.0).astype(jnp.float32)


def reorder(rows, to_tiles):
    return jnp.dot(
        rows, selector(to_tiles), precision=lax.Precision.HIGHEST, preferred_element_type=jnp.float32
    )


def prepare_kernel(source, cond, out, work):
    rows = jnp.concatenate([source[...].reshape(64, 512), cond[...].reshape(64, 512)], axis=0)
    tiles = reorder(rows, True)
    for c in range(4):
        work[c] = tiles[:, lanes(c)]
    for a in range(2):
        for z in range(4):
            for d in range(4):
                for c in range(4):
                    out[z, 4 * a + d, :, lanes(c)] = work[c, pl.ds(64 * a + 16 * z + d, 4, stride=4), :]


def finish_kernel(adjoint, remain, out_a, out_r, work):
    for a, ref in enumerate((adjoint, remain)):
        for z in range(4):
            for d in range(4):
                for c in range(4):
                    work[c, pl.ds(64 * a + 16 * z + d, 4, stride=4), :] = ref[z, d, :, lanes(c)]
    rows = reorder(jnp.concatenate([work[c] for c in range(4)], axis=1), False)
    out_a[...] = rows[0:64].reshape(4, 16, 512)
    out_r[...] = rows[64:128].reshape(4, 16, 512)


def fine_down_kernel(first, prm, chip, side, more, *refs):
    if first:
        rhs, field, low, cond, inv, wa, wb, dw = refs
    else:
        inv, rhs, field, low, wa, wb, dw = refs
    core = prm[0]

    def put(t, ref, *index):
        rhs[t] = ref[(*index, slice(0, 4))]
        if first:
            cond[t] = ref[(*index, slice(4, 8))]

    @pl.when(core == 0)
    def _():
        for t in range(6):
            put(t, side, 0, t)
        for t in range(8):
            put(6 + t, chip, t // 4, t % 4)
        for t in range(2):
            put(14 + t, more, 1, t)

    @pl.when(core == 1)
    def _():
        for t in range(2):
            put(t, more, 0, t)
        for t in range(8):
            put(2 + t, chip, t // 4, t % 4)
        for t in range(6):
            put(10 + t, side, 1, t)

    if first:

        def fill(t, carry):
            inv[t] = inverse_of(cond[t], SCALES[0])
            return carry

        lax.fori_loop(0, 16, fill, 0)
    steps = chebyshev(DEGREE)
    first_step(0, 16, rhs, inv, wa, dw, 4, steps[0][1])
    sweep(1, 15, wa, wb, 0, dw, rhs, inv, 0, 4, SCALES[0], *steps[1])
    sweep(2, 14, wb, field, -2, dw, rhs, inv, 0, 4, SCALES[0], *steps[2])
    for t in range(2):
        z = 6 + 2 * t
        one = residual_plane(field, z - 2, rhs, inv, z, 4, SCALES[0])
        two = residual_plane(field, z - 1, rhs, inv, z + 1, 4, SCALES[0])
        mean = halve(one, two, 4)
        for d in range(2):
            for c in range(2):
                low[0, t, d, :, lanes(c)] = mean[d][c][0:4]
        if first:
            mean = halve(load(cond, z, 4), load(cond, z + 1, 4), 4)
            for d in range(2):
                for c in range(2):
                    low[1, t, d, :, lanes(c)] = mean[d][c][0:4]


def middle_down_kernel(first, prm, chip, far, *refs):
    if first:
        rhs, field, low, cond, inv, wa, wb, dw = refs
    else:
        inv, rhs, field, low, wa, wb, dw = refs
    core, me = prm[0], prm[1]
    for j in range(8):
        y = lax.rem(me + j, 8)
        for t in range(12):
            if t < 4:
                ref, index = far, (0, t // 2, y)
            elif t < 8:
                ref, index = chip, ((t - 4) // 2, y)
            else:
                ref, index = far, (1, (t - 8) // 2, y)
            for d in range(2):
                rhs[t, d, 4 * j : 4 * j + 4, :] = ref[(*index, 0, t % 2, d)]
                if first:
                    cond[t, d, 4 * j : 4 * j + 4, :] = ref[(*index, 1, t % 2, d)]
    if first:

        def fill(t, carry):
            inv[t] = inverse_of(cond[t], SCALES[1])
            return carry

        lax.fori_loop(0, 12, fill, 0)
    steps = chebyshev(DEGREE)
    first_step(0, 12, rhs, inv, wa, dw, 2, steps[0][1])
    sweep(1, 11, wa, wb, 0, dw, rhs, inv, 0, 2, SCALES[1], *steps[1])
    sweep(2, 10, wb, field, -2, dw, rhs, inv, 0, 2, SCALES[1], *steps[2])
    z = 4 + 2 * core
    one = residual_plane(field, z - 2, rhs, inv, z, 2, SCALES[1])
    two = residual_plane(field, z - 1, rhs, inv, z + 1, 2, SCALES[1])
    low[0] = halve(one, two, 2)[0][0]
    if first:
        low[1] = halve(load(cond, z, 2), load(cond, z + 1, 2), 2)[0][0]


def coarse_kernel(first, prm, block, far, middle, mid_cond, *refs):
    if first:
        start, send, cond, inv, rhs, wa, wb, dw = refs
    else:
        cond, inv, start, send, rhs, wa, wb, dw = refs
    core, half = prm[0], prm[2]
    for t in range(12):
        if t < 4:
            ref, index = far, (0, t)
        elif t < 8:
            ref, index = block, (t - 4,)
        else:
            ref, index = far, (3, t - 8)
        rhs[t, 0] = ref[(*index, 0)]
        if first:
            value = ref[(*index, 1)]
            cond[t, 0] = value
            inv[t, 0] = inverse_of(value, SCALES[2])
    steps = chebyshev(COARSE_DEGREE)
    first_step(0, 12, rhs, inv, wa, dw, 1, steps[0][1])
    sweep(1, 11, wa, wb, 0, dw, rhs, inv, 0, 1, SCALES[2], *steps[1])
    sweep(2, 10, wb, wa, 0, dw, rhs, inv, 0, 1, SCALES[2], *steps[2])
    sweep(3, 9, wa, wb, 0, dw, rhs, inv, 0, 1, SCALES[2], *steps[3])
    for u in range(8):
        t = 3 + 2 * half + u // 2
        value = wb[t, 0] / cond[t, 0]
        value = jnp.concatenate([value[0:8], value[24:32]], axis=0)
        k = load_ends(mid_cond, u + 2, 2)
        w = load_ends(middle, u, 2)
        for d in range(2):
            for c in range(2):
                start[u, d, :, lanes(c)] = w[d][c] + k[d][c] * value
    for t in range(3):
        send[t] = start[4 - 3 * core + t]


def up_kernel(last, prm, start, side, more, mid_rhs, mid_cond, mid_inv, rhs, fine, cond, inv, *refs):
    if last:
        before, adjoint, remain, mid_a, mid_b, mid_dw, wa, wb, dw = refs
    else:
        adjoint, remain, mid_a, mid_b, mid_dw, wa, wb, dw = refs
    core = prm[0]

    @pl.when(core == 0)
    def _():
        for t in range(3):
            mid_a[t] = side[0, t]
        for t in range(8):
            mid_a[3 + t] = start[t]
        mid_a[11] = more[1]

    @pl.when(core == 1)
    def _():
        mid_a[0] = more[0]
        for t in range(8):
            mid_a[1 + t] = start[t]
        for t in range(3):
            mid_a[9 + t] = side[1, t]

    steps = chebyshev(DEGREE)
    shift = 2 * core - 1
    sweep(1, 11, mid_a, mid_b, 0, mid_dw, mid_rhs, mid_inv, shift, 2, SCALES[1], *steps[0], loader=load_ends)
    sweep(2, 10, mid_b, mid_a, 0, mid_dw, mid_rhs, mid_inv, shift, 2, SCALES[1], *steps[1], loader=load_ends)
    sweep(3, 9, mid_a, mid_b, 0, mid_dw, mid_rhs, mid_inv, shift, 2, SCALES[1], *steps[2], loader=load_ends)

    near = lax.broadcasted_iota(jnp.int32, (8, LANES), 0) < 6

    def correct(t, carry):
        k = load_ends(mid_cond, t + shift, 2)
        for d in range(2):
            for c in range(2):
                value = mid_b[t, d, :, lanes(c)] / k[d][c]
                value = jnp.where(near, value[0:8], value[8:16])
                for z in range(2):
                    v = 2 * (t - 3) + z
                    for dd in (2 * d, 2 * d + 1):
                        for cc in (2 * c, 2 * c + 1):
                            wa[v, dd, :, lanes(cc)] = fine[v, dd, :, lanes(cc)] + cond[v + 2, dd, :, lanes(cc)] * value
        return carry

    lax.fori_loop(3, 9, correct, 0)
    sweep(1, 11, wa, wb, 0, dw, rhs, inv, 2, 4, SCALES[0], *steps[0])
    sweep(2, 10, wb, wa, 0, dw, rhs, inv, 2, 4, SCALES[0], *steps[1])
    sweep(3, 9, wa, wb, 0, dw, rhs, inv, 2, 4, SCALES[0], *steps[2])

    def finish(t, carry):
        left = residual_plane(wb, t + 4, rhs, inv, t + 6, 4, SCALES[0])
        for d in range(4):
            for c in range(4):
                value = wb[t + 4, d, :, lanes(c)] / cond[t + 6, d, :, lanes(c)]
                value = value[0:4]
                if last:
                    value = value + before[t, d, :, lanes(c)]
                adjoint[t, d, :, lanes(c)] = value
                remain[t, d, :, lanes(c)] = left[d][c][0:4]
        return carry

    lax.fori_loop(0, 4, finish, 0)


def f32(*shape):
    return jax.ShapeDtypeStruct(shape, jnp.float32)


def call(body, outs, scratch, *args, scalars=True, name=None):
    specs = [pl.BlockSpec(memory_space=pltpu.VMEM)] * len(args)
    if scalars:
        specs[0] = pl.BlockSpec(memory_space=pltpu.SMEM)
    return pl.pallas_call(
        body,
        out_shape=outs,
        in_specs=specs,
        out_specs=[pl.BlockSpec(memory_space=pltpu.VMEM)] * len(outs),
        scratch_shapes=[pltpu.VMEM(s, jnp.float32) for s in scratch],
        compiler_params=pltpu.CompilerParams(vmem_limit_bytes=VMEM_LIMIT),
        name=name,
    )(*args)


def groups(axis, size, shift):
    devices = lax.axis_size(axis)
    return [[(g * size + i + shift) % devices for i in range(size)] for g in range(devices // size)]


def gather(value, size, shift):
    return lax.all_gather(value, "gz", axis_index_groups=groups("gz", size, shift))


def row_halo(own):
    devices = lax.axis_size("gy")
    up = [(i, (i + 1) % devices) for i in range(devices)]
    down = [(j, i) for i, j in up]
    after = lax.ppermute(own[:, :, 0:2], "gy", down)
    before = lax.ppermute(own[:, :, 2:4], "gy", up)
    return jnp.concatenate([own, after, before], axis=2)


def local(source, conduct):
    z = lax.axis_index("gz")
    y = lax.axis_index("gy")
    core = z % 2
    prm = jnp.stack([core, y, (z % 4) // 2, 0]).astype(jnp.int32)
    (remain,) = call(
        prepare_kernel, [f32(4, 8, 4, 512)], [(4, 128, 128)], source, conduct, scalars=False, name="prepare"
    )
    adjoint = None
    kept = None
    for cycle in range(CYCLES):
        first, last = cycle == 0, cycle == CYCLES - 1
        parts = 2 if first else 1
        own = row_halo(remain)
        chip = gather(own, 2, 0)
        whole = chip.reshape(8, *chip.shape[2:])
        side = gather(lax.dynamic_slice_in_dim(whole, 2 * core, 6, 0), 2, 1)
        flat = side.reshape(12, *side.shape[2:])
        more = gather(lax.dynamic_slice_in_dim(flat, 4 + 2 * core, 2, 0), 2, 0)
        outs = [f32(16, 4, 8, 512), f32(12, 4, 8, 512), f32(parts, 2, 2, 4, 256)]
        state = [f32(16, 4, 8, 512)] * 2
        scratch = [(16, 4, 8, 512)] * 3
        body = functools.partial(fine_down_kernel, first)
        if first:
            rhs0, field0, low, cond0, inv0 = call(
                body, outs + state, scratch, prm, chip, side, more, name="fine_down_first"
            )
        else:
            cond0, inv0 = kept[0:2]
            rhs0, field0, low = call(body, outs, scratch, prm, chip, side, more, inv0, name="fine_down")
        copies = jnp.broadcast_to(low, (lax.axis_size("gy"), *low.shape))
        rows = lax.all_to_all(copies, "gy", split_axis=0, concat_axis=0, tiled=True)
        chip = gather(rows, 2, 0)
        side = gather(chip, 2, 1)
        far = gather(lax.dynamic_index_in_dim(side, core, 0, keepdims=False), 2, 0)
        outs = [f32(12, 2, 32, 256), f32(8, 2, 32, 256), f32(parts, 32, 128)]
        state = [f32(12, 2, 32, 256)] * 2
        scratch = [(12, 2, 32, 256)] * 3
        body = functools.partial(middle_down_kernel, first)
        if first:
            rhs1, field1, low, cond1, inv1 = call(
                body, outs + state, scratch, prm, chip, far, name="middle_down_first"
            )
        else:
            cond1, inv1 = kept[2:4]
            rhs1, field1, low = call(body, outs, scratch, prm, chip, far, inv1, name="middle_down")
        block = gather(low, 4, 0)
        side = gather(block, 4, 2)
        half = prm[2]
        far = gather(lax.dynamic_index_in_dim(side, 2 * half, 0, keepdims=False), 4, 0)
        outs = [f32(8, 2, 16, 256), f32(3, 2, 16, 256)]
        state = [f32(12, 1, 32, 128)] * 2
        scratch = [(12, 1, 32, 128)] * 4
        body = functools.partial(coarse_kernel, first)
        if first:
            start, send, cond2, inv2 = call(
                body, outs + state, scratch, prm, block, far, field1, cond1, name="coarse_first"
            )
        else:
            cond2, inv2 = kept[4:6]
            start, send = call(
                body, outs, scratch, prm, block, far, field1, cond1, cond2, inv2, name="coarse"
            )
        side = gather(send, 2, 1)
        flat = side.reshape(6, *side.shape[2:])
        more = gather(lax.dynamic_index_in_dim(flat, 2 + core, 0, keepdims=False), 2, 0)
        outs = [f32(4, 4, 4, 512)] * 2
        scratch = [(12, 2, 16, 256)] * 3 + [(12, 4, 8, 512)] * 3
        args = [prm, start, side, more, rhs1, cond1, inv1, rhs0, field0, cond0, inv0]
        if last:
            args.append(adjoint)
        adjoint, remain = call(functools.partial(up_kernel, last), outs, scratch, *args, name="up")
        kept = (cond0, inv0, cond1, inv1, cond2, inv2)
    return tuple(
        call(
            finish_kernel,
            [f32(4, 16, 512)] * 2,
            [(4, 128, 128)],
            adjoint,
            remain,
            scalars=False,
            name="finish",
        )
    )


def solution(mesh):
    placed = (P("gz", "gy", None), P("gz", "gy", None))
    return jax.shard_map(local, mesh=mesh, in_specs=placed, out_specs=placed, check_vma=False)
```

```python
import functools

import jax
import jax.numpy as jnp
from jax import lax
from jax.experimental import pallas as pl
from jax.experimental.pallas import tpu as pltpu
from jax.sharding import PartitionSpec as P

DEGREE = 3
COARSE_DEGREE = 4
CYCLES = 2

CHEB_LOW = 0.3
CHEB_HIGH = 1.9
SCALES = (4.0, 1.0, 0.25)
LANES = 128
VMEM_LIMIT = 48 * 1024 * 1024


def chebyshev(steps):
    theta = (CHEB_HIGH + CHEB_LOW) / 2.0
    delta = (CHEB_HIGH - CHEB_LOW) / 2.0
    sigma = theta / delta
    rho = 1.0 / sigma
    pairs = [(0.0, 1.0 / theta)]
    for _ in range(steps - 1):
        rho_next = 1.0 / (2.0 * sigma - rho)
        pairs.append((rho_next * rho, 2.0 * rho_next / delta))
        rho = rho_next
    return pairs


def lanes(c):
    return slice(c * LANES, (c + 1) * LANES)


def load(ref, z, size):
    return [[ref[z, d, :, lanes(c)] for c in range(size)] for d in range(size)]


def load_ends(ref, z, size):
    top = ref.shape[2]
    return [
        [
            jnp.concatenate([ref[z, d, 0:8, lanes(c)], ref[z, d, top - 8 : top, lanes(c)]], axis=0)
            for c in range(size)
        ]
        for d in range(size)
    ]


def neighbours(below, here, above, size):
    rows = here[0][0].shape[0]
    lane = lax.broadcasted_iota(jnp.int32, (rows, LANES), 1)
    first, last = lane == 0, lane == LANES - 1
    out = []
    for d in range(size):
        line = []
        for c in range(size):
            if c > 0:
                left = here[d][c - 1]
            else:
                left = jnp.where(first, 0.0, pltpu.roll(here[d][size - 1], 1, 1))
            if c < size - 1:
                right = here[d][c + 1]
            else:
                right = jnp.where(last, 0.0, pltpu.roll(here[d][0], LANES - 1, 1))
            low = here[d - 1][c] if d > 0 else pltpu.roll(here[size - 1][c], 1, 0)
            high = here[d + 1][c] if d < size - 1 else pltpu.roll(here[0][c], rows - 1, 0)
            line.append(((below[d][c] + above[d][c]) + (left + right)) + (low + high))
        out.append(line)
    return out


def first_step(lo, hi, rhs, inv, w, dw, size, beta, group=1):
    def body(step, carry):
        for z in [lo + step * group + g for g in range(group)]:
            for d in range(size):
                for c in range(size):
                    value = (beta * rhs[z, d, :, lanes(c)]) * inv[z, d, :, lanes(c)]
                    w[z, d, :, lanes(c)] = value
                    dw[z, d, :, lanes(c)] = value
        return carry

    lax.fori_loop(0, (hi - lo) // group, body, 0)


def sweep(lo, hi, src, dst, dst_shift, dw, rhs, inv, shift, size, scale, alpha, beta, loader=load, group=1):
    def body(step, carry):
        start = lo + step * group
        planes = {g: load(src, start + g, size) for g in range(-1, group + 1)}
        done = []
        for g in range(group):
            z, here = start + g, planes[g]
            near = neighbours(planes[g - 1], here, planes[g + 1], size)
            f = loader(rhs, z + shift, size)
            i = loader(inv, z + shift, size)
            for d in range(size):
                for c in range(size):
                    q = i[d][c] * (f[d][c] + scale * near[d][c]) - here[d][c]
                    change = beta * q
                    if alpha != 0.0:
                        change = change + alpha * dw[z, d, :, lanes(c)]
                    done.append((z, d, c, change, here[d][c] + change))
        for z, d, c, change, value in done:
            dw[z, d, :, lanes(c)] = change
            dst[z + dst_shift, d, :, lanes(c)] = value
        return carry

    lax.fori_loop(0, (hi - lo) // group, body, 0)


def residual_plane(src, z, rhs, inv, zr, size, scale):
    here = load(src, z, size)
    near = neighbours(load(src, z - 1, size), here, load(src, z + 1, size), size)
    out = []
    for d in range(size):
        line = []
        for c in range(size):
            i = inv[zr, d, :, lanes(c)]
            line.append((rhs[zr, d, :, lanes(c)] + scale * near[d][c]) - here[d][c] / i)
        out.append(line)
    return out


def halve(one, two, size):
    half = size // 2
    return [
        [
            0.125
            * (
                ((one[2 * d][2 * c] + one[2 * d][2 * c + 1]) + (one[2 * d + 1][2 * c] + one[2 * d + 1][2 * c + 1]))
                + ((two[2 * d][2 * c] + two[2 * d][2 * c + 1]) + (two[2 * d + 1][2 * c] + two[2 * d + 1][2 * c + 1]))
            )
            for c in range(half)
        ]
        for d in range(half)
    ]


def inverse_of(cond, scale):
    return 1.0 / (1.0 / cond + 6.0 * scale)


def selector(to_tiles):
    rows = lax.broadcasted_iota(jnp.int32, (512, 512), 0)
    cols = lax.broadcasted_iota(jnp.int32, (512, 512), 1)
    if to_tiles:
        hit = rows == 4 * (cols % LANES) + cols // LANES
    else:
        hit = cols == 4 * (rows % LANES) + rows // LANES
    return jnp.where(hit, 1.0, 0.0).astype(jnp.float32)


def reorder(rows, to_tiles):
    return jnp.dot(
        rows, selector(to_tiles), precision=lax.Precision.HIGHEST, preferred_element_type=jnp.float32
    )


def prepare_kernel(source, cond, out, work):
    rows = jnp.concatenate([source[...].reshape(64, 512), cond[...].reshape(64, 512)], axis=0)
    tiles = reorder(rows, True)
    for c in range(4):
        work[c] = tiles[:, lanes(c)]
    for a in range(2):
        for z in range(4):
            for d in range(4):
                for c in range(4):
                    out[z, 4 * a + d, :, lanes(c)] = work[c, pl.ds(64 * a + 16 * z + d, 4, stride=4), :]


def finish_kernel(adjoint, remain, out_a, out_r, work):
    for a, ref in enumerate((adjoint, remain)):
        for z in range(4):
            for d in range(4):
                for c in range(4):
                    work[c, pl.ds(64 * a + 16 * z + d, 4, stride=4), :] = ref[z, d, :, lanes(c)]
    rows = reorder(jnp.concatenate([work[c] for c in range(4)], axis=1), False)
    out_a[...] = rows[0:64].reshape(4, 16, 512)
    out_r[...] = rows[64:128].reshape(4, 16, 512)


def rows_kernel(parts, prm, chip, halves, *outs):
    core, odd = prm[0], prm[1]
    for a in range(parts):
        whole, send = outs[2 * a : 2 * a + 2]
        for t in range(8):
            for d in range(4):
                whole[t, d, 0:4, :] = chip[t // 4, t % 4, 4 * a + d]
                whole[t, d, 4:6, :] = halves[odd, t, 4 * a + d]
                whole[t, d, 6:8, :] = halves[1 - odd, t, 4 * a + d]
        for t in range(6):
            send[t] = whole[2 * core + t]


def fine_down_kernel(first, prm, *refs):
    if first:
        whole, side, whole_k, side_k, more, more_k, rhs, field, low, cond, inv, wa, wb, dw = refs
    else:
        whole, side, more, inv, rhs, field, low, wa, wb, dw = refs
    core = prm[0]

    def assemble(out, own, beside, beyond):
        @pl.when(core == 0)
        def _():
            for t in range(6):
                out[t] = beside[0, t]
            for t in range(8):
                out[6 + t] = own[t]
            for t in range(2):
                out[14 + t] = beyond[1, t]

        @pl.when(core == 1)
        def _():
            for t in range(2):
                out[t] = beyond[0, t]
            for t in range(8):
                out[2 + t] = own[t]
            for t in range(6):
                out[10 + t] = beside[1, t]

    assemble(rhs, whole, side, more)
    if first:
        assemble(cond, whole_k, side_k, more_k)

    if first:

        def fill(t, carry):
            inv[t] = inverse_of(cond[t], SCALES[0])
            return carry

        lax.fori_loop(0, 16, fill, 0)
    steps = chebyshev(DEGREE)
    first_step(0, 16, rhs, inv, wa, dw, 4, steps[0][1])
    sweep(1, 15, wa, wb, 0, dw, rhs, inv, 0, 4, SCALES[0], *steps[1])
    sweep(2, 14, wb, field, -2, dw, rhs, inv, 0, 4, SCALES[0], *steps[2])
    for t in range(2):
        z = 6 + 2 * t
        one = residual_plane(field, z - 2, rhs, inv, z, 4, SCALES[0])
        two = residual_plane(field, z - 1, rhs, inv, z + 1, 4, SCALES[0])
        mean = halve(one, two, 4)
        for d in range(2):
            for c in range(2):
                low[0, t, d, :, lanes(c)] = mean[d][c][0:4]
        if first:
            mean = halve(load(cond, z, 4), load(cond, z + 1, 4), 4)
            for d in range(2):
                for c in range(2):
                    low[1, t, d, :, lanes(c)] = mean[d][c][0:4]


def pick_kernel(prm, rows, out):
    for j, step in enumerate((0, 1, 2, 6, 7)):
        out[j] = rows[lax.rem(prm[2] + step, 8)]


def middle_down_kernel(first, prm, chip, far, *refs):
    if first:
        rhs, field, low, cond, inv, wa, wb, dw = refs
    else:
        inv, rhs, field, low, wa, wb, dw = refs
    for t in range(12):
        if t < 4:
            ref, at = far.at[0], t
        elif t < 8:
            ref, at = chip, t - 4
        else:
            ref, at = far.at[1], t - 8
        for d in range(2):
            for j, row in enumerate((0, 4, 8, 16, 20)):
                rhs[t, d, row : row + 4, :] = ref[at // 2, j, 0, at % 2, d]
                if first:
                    cond[t, d, row : row + 4, :] = ref[at // 2, j, 1, at % 2, d]
            rhs[t, d, 12:16, :] = jnp.zeros((4, 256), jnp.float32)
            if first:
                cond[t, d, 12:16, :] = jnp.ones((4, 256), jnp.float32)
    if first:

        def fill(t, carry):
            inv[t] = inverse_of(cond[t], SCALES[1])
            return carry

        lax.fori_loop(0, 12, fill, 0)
    steps = chebyshev(DEGREE)
    first_step(0, 12, rhs, inv, wa, dw, 2, steps[0][1], group=2)
    sweep(1, 11, wa, wb, 0, dw, rhs, inv, 0, 2, SCALES[1], *steps[1], group=2)
    sweep(2, 10, wb, field, -2, dw, rhs, inv, 0, 2, SCALES[1], *steps[2], group=2)
    for h in range(2):
        z = 4 + 2 * h
        one = residual_plane(field, z - 2, rhs, inv, z, 2, SCALES[1])
        two = residual_plane(field, z - 1, rhs, inv, z + 1, 2, SCALES[1])
        low[0, h] = halve(one, two, 2)[0][0]
        if first:
            low[1, h] = halve(load(cond, z, 2), load(cond, z + 1, 2), 2)[0][0]


def coarse_kernel(first, prm, block, far, middle, mid_cond, *refs):
    if first:
        start, send, cond, inv, rhs, wa, wb, dw = refs
    else:
        cond, inv, start, send, rhs, wa, wb, dw = refs
    core, half = prm[0], prm[3]
    for t in range(12):
        if t < 4:
            ref, at = far.at[0], t
        elif t < 8:
            ref, at = block, t - 4
        else:
            ref, at = far.at[1], t - 8
        rhs[t, 0] = ref[at // 2, 0, at % 2]
        if first:
            value = ref[at // 2, 1, at % 2]
            cond[t, 0] = value
            inv[t, 0] = inverse_of(value, SCALES[2])
    steps = chebyshev(COARSE_DEGREE)
    first_step(0, 12, rhs, inv, wa, dw, 1, steps[0][1], group=12)
    sweep(1, 11, wa, wb, 0, dw, rhs, inv, 0, 1, SCALES[2], *steps[1], group=10)
    sweep(2, 10, wb, wa, 0, dw, rhs, inv, 0, 1, SCALES[2], *steps[2], group=8)
    sweep(3, 9, wa, wb, 0, dw, rhs, inv, 0, 1, SCALES[2], *steps[3], group=6)
    for u in range(8):
        t = 3 + 2 * half + u // 2
        value = wb[t, 0] / cond[t, 0]
        value = jnp.concatenate([value[0:8], value[16:24]], axis=0)
        k = load_ends(mid_cond, u + 2, 2)
        w = load_ends(middle, u, 2)
        for d in range(2):
            for c in range(2):
                start[u, d, :, lanes(c)] = w[d][c] + k[d][c] * value
    for t in range(3):
        send[t] = start[4 - 3 * core + t]


def up_kernel(last, prm, start, side, more, mid_rhs, mid_cond, mid_inv, rhs, fine, cond, inv, *refs):
    if last:
        before, adjoint, remain, mid_a, mid_b, mid_dw, wa, wb, dw = refs
    else:
        adjoint, remain, mid_a, mid_b, mid_dw, wa, wb, dw = refs
    core = prm[0]

    @pl.when(core == 0)
    def _():
        for t in range(3):
            mid_a[t] = side[0, t]
        for t in range(8):
            mid_a[3 + t] = start[t]
        mid_a[11] = more[1]

    @pl.when(core == 1)
    def _():
        mid_a[0] = more[0]
        for t in range(8):
            mid_a[1 + t] = start[t]
        for t in range(3):
            mid_a[9 + t] = side[1, t]

    steps = chebyshev(DEGREE)
    shift = 2 * core - 1
    sweep(1, 11, mid_a, mid_b, 0, mid_dw, mid_rhs, mid_inv, shift, 2, SCALES[1], *steps[0], loader=load_ends, group=2)
    sweep(2, 10, mid_b, mid_a, 0, mid_dw, mid_rhs, mid_inv, shift, 2, SCALES[1], *steps[1], loader=load_ends, group=2)
    sweep(3, 9, mid_a, mid_b, 0, mid_dw, mid_rhs, mid_inv, shift, 2, SCALES[1], *steps[2], loader=load_ends, group=2)

    near = lax.broadcasted_iota(jnp.int32, (8, LANES), 0) < 6

    def correct(t, carry):
        k = load_ends(mid_cond, t + shift, 2)
        for d in range(2):
            for c in range(2):
                value = mid_b[t, d, :, lanes(c)] / k[d][c]
                value = jnp.where(near, value[0:8], value[8:16])
                for z in range(2):
                    v = 2 * (t - 3) + z
                    for dd in (2 * d, 2 * d + 1):
                        for cc in (2 * c, 2 * c + 1):
                            wa[v, dd, :, lanes(cc)] = fine[v, dd, :, lanes(cc)] + cond[v + 2, dd, :, lanes(cc)] * value
        return carry

    lax.fori_loop(3, 9, correct, 0)
    sweep(1, 11, wa, wb, 0, dw, rhs, inv, 2, 4, SCALES[0], *steps[0])
    sweep(2, 10, wb, wa, 0, dw, rhs, inv, 2, 4, SCALES[0], *steps[1])
    sweep(3, 9, wa, wb, 0, dw, rhs, inv, 2, 4, SCALES[0], *steps[2])

    def finish(t, carry):
        left = residual_plane(wb, t + 4, rhs, inv, t + 6, 4, SCALES[0])
        for d in range(4):
            for c in range(4):
                value = wb[t + 4, d, :, lanes(c)] / cond[t + 6, d, :, lanes(c)]
                value = value[0:4]
                if last:
                    value = value + before[t, d, :, lanes(c)]
                adjoint[t, d, :, lanes(c)] = value
                remain[t, d, :, lanes(c)] = left[d][c][0:4]
        return carry

    lax.fori_loop(0, 4, finish, 0)


def f32(*shape):
    return jax.ShapeDtypeStruct(shape, jnp.float32)


def call(body, outs, scratch, *args, scalars=True, name=None):
    specs = [pl.BlockSpec(memory_space=pltpu.VMEM)] * len(args)
    if scalars:
        specs[0] = pl.BlockSpec(memory_space=pltpu.SMEM)
    return pl.pallas_call(
        body,
        out_shape=outs,
        in_specs=specs,
        out_specs=[pl.BlockSpec(memory_space=pltpu.VMEM)] * len(outs),
        scratch_shapes=[pltpu.VMEM(s, jnp.float32) for s in scratch],
        compiler_params=pltpu.CompilerParams(vmem_limit_bytes=VMEM_LIMIT),
        name=name,
    )(*args)


def pairs(first, step, size):
    devices = lax.axis_size("gz")
    return [[(b + i) % devices, (b + i + step) % devices] for b in range(0, devices, size) for i in first]


def gather(value, first, step, size):
    return lax.all_gather(value, "gz", axis_index_groups=pairs(first, step, size))


def cores(value):
    return gather(value, (0,), 1, 2)


def across(value):
    return gather(value, (1,), 1, 2)


def row_pairs(value):
    planes, rows = lax.axis_size("gz"), lax.axis_size("gy")
    members = []
    for z in range(planes):
        for y in range(z % 2, rows, 2):
            members.append([z * rows + y, z * rows + (y + 1) % rows])
    return lax.all_gather(value, ("gz", "gy"), axis_index_groups=members)


def pick(value, index):
    return lax.dynamic_index_in_dim(value, index, 0, keepdims=False)


def local(source, conduct):
    z = lax.axis_index("gz")
    y = lax.axis_index("gy")
    core = z % 2
    half = (z % 4) // 2
    prm = jnp.stack([core, y % 2, y, half]).astype(jnp.int32)
    place = (core + y) % 2
    (remain,) = call(
        prepare_kernel, [f32(4, 8, 4, 512)], [(4, 128, 128)], source, conduct, scalars=False, name="prepare"
    )
    adjoint = None
    kept = None
    for cycle in range(CYCLES):
        first, last = cycle == 0, cycle == CYCLES - 1
        parts = 2 if first else 1
        chip = cores(remain)
        flat = chip.reshape(8, *chip.shape[2:])
        halves = row_pairs(jnp.where(place == 0, flat[:, :, 2:4], flat[:, :, 0:2]))
        halves = cores(jnp.where(place == 0, halves[1], halves[0]))
        laid = call(
            functools.partial(rows_kernel, parts),
            [f32(8, 4, 8, 512), f32(6, 4, 8, 512)] * parts,
            [],
            prm,
            chip,
            halves,
            name="rows",
        )
        args, mores = [prm], []
        for a in range(parts):
            side = across(laid[2 * a + 1])
            args += [laid[2 * a], side]
            flat = side.reshape(12, *side.shape[2:])
            mores.append(cores(lax.dynamic_slice_in_dim(flat, 4 + 2 * core, 2, 0)))
        args += mores
        outs = [f32(16, 4, 8, 512), f32(12, 4, 8, 512), f32(parts, 2, 2, 4, 256)]
        state = [f32(16, 4, 8, 512)] * 2
        scratch = [(16, 4, 8, 512)] * 3
        body = functools.partial(fine_down_kernel, first)
        if first:
            rhs0, field0, low, cond0, inv0 = call(body, outs + state, scratch, *args, name="fine_down_first")
        else:
            cond0, inv0 = kept[0:2]
            rhs0, field0, low = call(body, outs, scratch, *args, inv0, name="fine_down")
        copies = jnp.broadcast_to(low, (lax.axis_size("gy"), *low.shape))
        rows = lax.all_to_all(copies, "gy", split_axis=0, concat_axis=0, tiled=True)
        (rows,) = call(pick_kernel, [f32(5, parts, 2, 2, 4, 256)], [], prm, rows, name="pick")
        chip = cores(rows)
        far = cores(pick(across(chip), core))
        outs = [f32(12, 2, 24, 256), f32(8, 2, 24, 256), f32(parts, 2, 24, 128)]
        state = [f32(12, 2, 24, 256)] * 2
        scratch = [(12, 2, 24, 256)] * 3
        body = functools.partial(middle_down_kernel, first)
        if first:
            rhs1, field1, low, cond1, inv1 = call(
                body, outs + state, scratch, prm, chip, far, name="middle_down_first"
            )
        else:
            cond1, inv1 = kept[2:4]
            rhs1, field1, low = call(body, outs, scratch, prm, chip, far, inv1, name="middle_down")
        block = gather(low, (0, 1), 2, 4)
        side = gather(block, (2, 3), 2, 4)
        far = gather(pick(side, half), (0, 1), 2, 4)
        outs = [f32(8, 2, 16, 256), f32(3, 2, 16, 256)]
        state = [f32(12, 1, 24, 128)] * 2
        scratch = [(12, 1, 24, 128)] * 4
        body = functools.partial(coarse_kernel, first)
        if first:
            start, send, cond2, inv2 = call(
                body, outs + state, scratch, prm, block, far, field1, cond1, name="coarse_first"
            )
        else:
            cond2, inv2 = kept[4:6]
            start, send = call(
                body, outs, scratch, prm, block, far, field1, cond1, cond2, inv2, name="coarse"
            )
        side = across(send)
        more = cores(pick(side.reshape(6, *side.shape[2:]), 2 + core))
        outs = [f32(4, 4, 4, 512)] * 2
        scratch = [(12, 2, 16, 256)] * 3 + [(12, 4, 8, 512)] * 3
        args = [prm, start, side, more, rhs1, cond1, inv1, rhs0, field0, cond0, inv0]
        if last:
            args.append(adjoint)
        adjoint, remain = call(functools.partial(up_kernel, last), outs, scratch, *args, name="up")
        kept = (cond0, inv0, cond1, inv1, cond2, inv2)
    return tuple(
        call(
            finish_kernel,
            [f32(4, 16, 512)] * 2,
            [(4, 128, 128)],
            adjoint,
            remain,
            scalars=False,
            name="finish",
        )
    )


def solution(mesh):
    placed = (P("gz", "gy", None), P("gz", "gy", None))
    return jax.shard_map(local, mesh=mesh, in_specs=placed, out_specs=placed, check_vma=False)
```

```python
import functools

import jax
import jax.numpy as jnp
from jax import lax
from jax.experimental import pallas as pl
from jax.experimental.pallas import tpu as pltpu
from jax.sharding import PartitionSpec as P

DEGREE = 3
COARSE_DEGREE = 4
CYCLES = 2

CHEB_LOW = 0.3
CHEB_HIGH = 1.9
SCALES = (4.0, 1.0, 0.25)
LANES = 128
VMEM_LIMIT = 16 * 1024 * 1024


def chebyshev(steps):
    theta = (CHEB_HIGH + CHEB_LOW) / 2.0
    delta = (CHEB_HIGH - CHEB_LOW) / 2.0
    sigma = theta / delta
    rho = 1.0 / sigma
    pairs = [(0.0, 1.0 / theta)]
    for _ in range(steps - 1):
        rho_next = 1.0 / (2.0 * sigma - rho)
        pairs.append((rho_next * rho, 2.0 * rho_next / delta))
        rho = rho_next
    return pairs


def lanes(c):
    return slice(c * LANES, (c + 1) * LANES)


def load(ref, z, size):
    return [[ref[z, d, :, lanes(c)] for c in range(size)] for d in range(size)]


def load_ends(ref, z, size):
    top = ref.shape[2]
    return [
        [
            jnp.concatenate([ref[z, d, 0:8, lanes(c)], ref[z, d, top - 8 : top, lanes(c)]], axis=0)
            for c in range(size)
        ]
        for d in range(size)
    ]


def neighbours(below, here, above, size):
    rows = here[0][0].shape[0]
    lane = lax.broadcasted_iota(jnp.int32, (rows, LANES), 1)
    first, last = lane == 0, lane == LANES - 1
    out = []
    for d in range(size):
        line = []
        for c in range(size):
            if c > 0:
                left = here[d][c - 1]
            else:
                left = jnp.where(first, 0.0, pltpu.roll(here[d][size - 1], 1, 1))
            if c < size - 1:
                right = here[d][c + 1]
            else:
                right = jnp.where(last, 0.0, pltpu.roll(here[d][0], LANES - 1, 1))
            low = here[d - 1][c] if d > 0 else pltpu.roll(here[size - 1][c], 1, 0)
            high = here[d + 1][c] if d < size - 1 else pltpu.roll(here[0][c], rows - 1, 0)
            line.append(((below[d][c] + above[d][c]) + (left + right)) + (low + high))
        out.append(line)
    return out


def first_step(lo, hi, rhs, inv, w, dw, size, beta, group=1):
    def body(step, carry):
        for z in [lo + step * group + g for g in range(group)]:
            for d in range(size):
                for c in range(size):
                    value = (beta * rhs[z, d, :, lanes(c)]) * inv[z, d, :, lanes(c)]
                    w[z, d, :, lanes(c)] = value
                    dw[z, d, :, lanes(c)] = value
        return carry

    lax.fori_loop(0, (hi - lo) // group, body, 0)


def sweep(lo, hi, src, dst, dst_shift, dw, rhs, inv, shift, size, scale, alpha, beta, loader=load, group=1):
    def body(step, carry):
        start = lo + step * group
        planes = {g: load(src, start + g, size) for g in range(-1, group + 1)}
        done = []
        for g in range(group):
            z, here = start + g, planes[g]
            near = neighbours(planes[g - 1], here, planes[g + 1], size)
            f = loader(rhs, z + shift, size)
            i = loader(inv, z + shift, size)
            for d in range(size):
                for c in range(size):
                    q = i[d][c] * (f[d][c] + scale * near[d][c]) - here[d][c]
                    change = beta * q
                    if alpha != 0.0:
                        change = change + alpha * dw[z, d, :, lanes(c)]
                    done.append((z, d, c, change, here[d][c] + change))
        for z, d, c, change, value in done:
            dw[z, d, :, lanes(c)] = change
            dst[z + dst_shift, d, :, lanes(c)] = value
        return carry

    lax.fori_loop(0, (hi - lo) // group, body, 0)


def residual_plane(src, z, rhs, inv, zr, size, scale):
    here = load(src, z, size)
    near = neighbours(load(src, z - 1, size), here, load(src, z + 1, size), size)
    out = []
    for d in range(size):
        line = []
        for c in range(size):
            i = inv[zr, d, :, lanes(c)]
            line.append((rhs[zr, d, :, lanes(c)] + scale * near[d][c]) - here[d][c] / i)
        out.append(line)
    return out


def halve(one, two, size):
    half = size // 2
    return [
        [
            0.125
            * (
                ((one[2 * d][2 * c] + one[2 * d][2 * c + 1]) + (one[2 * d + 1][2 * c] + one[2 * d + 1][2 * c + 1]))
                + ((two[2 * d][2 * c] + two[2 * d][2 * c + 1]) + (two[2 * d + 1][2 * c] + two[2 * d + 1][2 * c + 1]))
            )
            for c in range(half)
        ]
        for d in range(half)
    ]


def inverse_of(cond, scale):
    return 1.0 / (1.0 / cond + 6.0 * scale)


def selector(to_tiles):
    rows = lax.broadcasted_iota(jnp.int32, (512, 512), 0)
    cols = lax.broadcasted_iota(jnp.int32, (512, 512), 1)
    if to_tiles:
        hit = rows == 4 * (cols % LANES) + cols // LANES
    else:
        hit = cols == 4 * (rows % LANES) + rows // LANES
    return jnp.where(hit, 1.0, 0.0).astype(jnp.float32)


def reorder(rows, to_tiles):
    return jnp.dot(
        rows, selector(to_tiles), precision=lax.Precision.HIGHEST, preferred_element_type=jnp.float32
    )


def prepare_kernel(source, cond, out, work):
    rows = jnp.concatenate([source[...].reshape(64, 512), cond[...].reshape(64, 512)], axis=0)
    tiles = reorder(rows, True)
    for c in range(4):
        work[c] = tiles[:, lanes(c)]
    for a in range(2):
        for z in range(4):
            for d in range(4):
                for c in range(4):
                    out[z, 4 * a + d, :, lanes(c)] = work[c, pl.ds(64 * a + 16 * z + d, 4, stride=4), :]


def finish_kernel(adjoint, remain, out_a, out_r, work):
    for a, ref in enumerate((adjoint, remain)):
        for z in range(4):
            for d in range(4):
                for c in range(4):
                    work[c, pl.ds(64 * a + 16 * z + d, 4, stride=4), :] = ref[z, d, :, lanes(c)]
    rows = reorder(jnp.concatenate([work[c] for c in range(4)], axis=1), False)
    out_a[...] = rows[0:64].reshape(4, 16, 512)
    out_r[...] = rows[64:128].reshape(4, 16, 512)


def rows_kernel(parts, prm, chip, halves, *outs):
    core, odd = prm[0], prm[1]
    for a in range(parts):
        whole, send = outs[2 * a : 2 * a + 2]
        for t in range(8):
            for d in range(4):
                whole[t, d, 0:4, :] = chip[t // 4, t % 4, 4 * a + d]
                whole[t, d, 4:6, :] = halves[odd, t, 4 * a + d]
                whole[t, d, 6:8, :] = halves[1 - odd, t, 4 * a + d]
        for t in range(6):
            send[t] = whole[2 * core + t]


def fine_down_kernel(first, prm, *refs):
    if first:
        whole, side, whole_k, side_k, rhs, field, low, edge, cond, inv, wa, wb, dw = refs
    else:
        whole, side, inv, rhs, field, low, edge, wa, wb, dw = refs
    core = prm[0]

    @pl.when(core == 0)
    def _():
        for t in range(6):
            rhs[t] = side[0, t]
            if first:
                cond[t] = side_k[t]
        for t in range(8):
            rhs[6 + t] = whole[t]
            if first:
                cond[6 + t] = whole_k[t]

    @pl.when(core == 1)
    def _():
        for t in range(8):
            rhs[t] = whole[t]
            if first:
                cond[t] = whole_k[t]
        for t in range(6):
            rhs[8 + t] = side[1, t]
            if first:
                cond[8 + t] = side_k[t]

    if first:

        def fill(t, carry):
            inv[t] = inverse_of(cond[t], SCALES[0])
            return carry

        lax.fori_loop(0, 14, fill, 0)
    steps = chebyshev(DEGREE)
    first_step(0, 14, rhs, inv, wa, dw, 4, steps[0][1])
    sweep(1, 13, wa, wb, 0, dw, rhs, inv, 0, 4, SCALES[0], *steps[1])
    sweep(2, 12, wb, field, -2, dw, rhs, inv, 0, 4, SCALES[0], *steps[2])
    for q in range(2):
        for d in range(4):
            for c in range(4):
                row = 8 * ((q * 4 + d) * 4 + c)
                edge[row : row + 8, :] = field[4 + q, d, :, lanes(c)]
    for t in range(2):
        z = 6 - 2 * core + 2 * t
        one = residual_plane(field, z - 2, rhs, inv, z, 4, SCALES[0])
        two = residual_plane(field, z - 1, rhs, inv, z + 1, 4, SCALES[0])
        mean = halve(one, two, 4)
        for d in range(2):
            for c in range(2):
                low[0, t, d, :, lanes(c)] = mean[d][c][0:4]
        if first:
            mean = halve(load(cond, z, 4), load(cond, z + 1, 4), 4)
            for d in range(2):
                for c in range(2):
                    low[1, t, d, :, lanes(c)] = mean[d][c][0:4]


def pick_kernel(prm, rows, out):
    for j, step in enumerate((0, 1, 2, 6, 7)):
        out[j] = rows[lax.rem(prm[2] + step, 8)]


def middle_down_kernel(first, prm, chip, far, *refs):
    if first:
        rhs, field, low, cond, inv, wa, wb, dw = refs
    else:
        inv, rhs, field, low, wa, wb, dw = refs
    for t in range(12):
        if t < 4:
            ref, at = far.at[0], t
        elif t < 8:
            ref, at = chip, t - 4
        else:
            ref, at = far.at[1], t - 8
        for d in range(2):
            for j, row in enumerate((0, 4, 8, 16, 20)):
                rhs[t, d, row : row + 4, :] = ref[at // 2, j, 0, at % 2, d]
                if first:
                    cond[t, d, row : row + 4, :] = ref[at // 2, j, 1, at % 2, d]
            rhs[t, d, 12:16, :] = jnp.zeros((4, 256), jnp.float32)
            if first:
                cond[t, d, 12:16, :] = jnp.ones((4, 256), jnp.float32)
    if first:

        def fill(t, carry):
            inv[t] = inverse_of(cond[t], SCALES[1])
            return carry

        lax.fori_loop(0, 12, fill, 0)
    steps = chebyshev(DEGREE)
    first_step(0, 12, rhs, inv, wa, dw, 2, steps[0][1], group=2)
    sweep(1, 11, wa, wb, 0, dw, rhs, inv, 0, 2, SCALES[1], *steps[1], group=2)
    sweep(2, 10, wb, field, -2, dw, rhs, inv, 0, 2, SCALES[1], *steps[2], group=2)
    for h in range(2):
        z = 4 + 2 * h
        one = residual_plane(field, z - 2, rhs, inv, z, 2, SCALES[1])
        two = residual_plane(field, z - 1, rhs, inv, z + 1, 2, SCALES[1])
        low[0, h] = halve(one, two, 2)[0][0]
        if first:
            low[1, h] = halve(load(cond, z, 2), load(cond, z + 1, 2), 2)[0][0]


def coarse_kernel(first, prm, block, far, middle, mid_cond, *refs):
    if first:
        start, send, cond, inv, rhs, wa, wb, dw = refs
    else:
        cond, inv, start, send, rhs, wa, wb, dw = refs
    core = prm[0]
    parts = 2 if first else 1
    for a in range(parts):
        for t in range(10):
            if t < 4:
                row = 256 + 48 * (a + parts * (1 - t // 2)) + 24 * (t % 2)
                value = far[0, row : row + 24, :]
            elif t < 6:
                value = block[a, t - 4]
            else:
                row = 256 + 48 * (a + parts * (t // 2 - 3)) + 24 * (t % 2)
                value = far[1, row : row + 24, :]
            if a == 0:
                rhs[t, 0] = value
            else:
                cond[t, 0] = value
                inv[t, 0] = inverse_of(value, SCALES[2])
    steps = chebyshev(COARSE_DEGREE)
    first_step(0, 10, rhs, inv, wa, dw, 1, steps[0][1], group=10)
    sweep(1, 9, wa, wb, 0, dw, rhs, inv, 0, 1, SCALES[2], *steps[1], group=8)
    sweep(2, 8, wb, wa, 0, dw, rhs, inv, 0, 1, SCALES[2], *steps[2], group=6)
    sweep(3, 7, wa, wb, 0, dw, rhs, inv, 0, 1, SCALES[2], *steps[3], group=4)
    for u in range(8):
        t = 3 + u // 2
        value = wb[t, 0] / cond[t, 0]
        value = jnp.concatenate([value[0:8], value[16:24]], axis=0)
        k = load_ends(mid_cond, u + 2, 2)
        w = load_ends(middle, u, 2)
        for d in range(2):
            for c in range(2):
                start[u, d, :, lanes(c)] = w[d][c] + k[d][c] * value
    for t in range(3):
        send[t] = start[4 - 3 * core + t]


def up_kernel(last, prm, start, side, more, far, mid_rhs, mid_cond, mid_inv, rhs, fine, cond, inv, *refs):
    if last:
        before, adjoint, remain, mid_a, mid_b, mid_dw, wa, wb, dw = refs
    else:
        adjoint, remain, mid_a, mid_b, mid_dw, wa, wb, dw = refs
    core = prm[0]

    def beyond(other, at):
        for q in range(2):
            for d in range(4):
                for c in range(4):
                    row = 8 * ((q * 4 + d) * 4 + c)
                    wa[at + q, d, :, lanes(c)] = far[other, row : row + 8, :]

    @pl.when(core == 0)
    def _():
        for t in range(3):
            mid_a[t] = side[0, t]
        for t in range(8):
            mid_a[3 + t] = start[t]
        mid_a[11] = more[1]
        for t in range(10):
            wa[t] = fine[t]
        beyond(1, 10)

    @pl.when(core == 1)
    def _():
        mid_a[0] = more[0]
        for t in range(8):
            mid_a[1 + t] = start[t]
        for t in range(3):
            mid_a[9 + t] = side[1, t]
        for t in range(10):
            wa[2 + t] = fine[t]
        beyond(0, 0)

    steps = chebyshev(DEGREE)
    shift = 2 * core - 1
    sweep(1, 11, mid_a, mid_b, 0, mid_dw, mid_rhs, mid_inv, shift, 2, SCALES[1], *steps[0], loader=load_ends, group=2)
    sweep(2, 10, mid_b, mid_a, 0, mid_dw, mid_rhs, mid_inv, shift, 2, SCALES[1], *steps[1], loader=load_ends, group=2)
    sweep(3, 9, mid_a, mid_b, 0, mid_dw, mid_rhs, mid_inv, shift, 2, SCALES[1], *steps[2], loader=load_ends, group=2)

    near = lax.broadcasted_iota(jnp.int32, (8, LANES), 0) < 6
    ahead = 2 - 2 * core

    def correct(t, carry):
        k = load_ends(mid_cond, t + shift, 2)
        for d in range(2):
            for c in range(2):
                value = mid_b[t, d, :, lanes(c)] / k[d][c]
                value = jnp.where(near, value[0:8], value[8:16])
                for z in range(2):
                    v = 2 * (t - 3) + z
                    for dd in (2 * d, 2 * d + 1):
                        for cc in (2 * c, 2 * c + 1):
                            wa[v, dd, :, lanes(cc)] = (
                                wa[v, dd, :, lanes(cc)] + cond[v + ahead, dd, :, lanes(cc)] * value
                            )
        return carry

    lax.fori_loop(3, 9, correct, 0)
    sweep(1, 11, wa, wb, 0, dw, rhs, inv, ahead, 4, SCALES[0], *steps[0])
    sweep(2, 10, wb, wa, 0, dw, rhs, inv, ahead, 4, SCALES[0], *steps[1])
    sweep(3, 9, wa, wb, 0, dw, rhs, inv, ahead, 4, SCALES[0], *steps[2])

    def finish(t, carry):
        left = residual_plane(wb, t + 4, rhs, inv, t + 4 + ahead, 4, SCALES[0])
        for d in range(4):
            for c in range(4):
                value = wb[t + 4, d, :, lanes(c)] / cond[t + 4 + ahead, d, :, lanes(c)]
                value = value[0:4]
                if last:
                    value = value + before[t, d, :, lanes(c)]
                adjoint[t, d, :, lanes(c)] = value
                remain[t, d, :, lanes(c)] = left[d][c][0:4]
        return carry

    lax.fori_loop(0, 4, finish, 0)


def f32(*shape):
    return jax.ShapeDtypeStruct(shape, jnp.float32)


def call(body, outs, scratch, *args, scalars=True, name=None):
    specs = [pl.BlockSpec(memory_space=pltpu.VMEM)] * len(args)
    if scalars:
        specs[0] = pl.BlockSpec(memory_space=pltpu.SMEM)
    return pl.pallas_call(
        body,
        out_shape=outs,
        in_specs=specs,
        out_specs=[pl.BlockSpec(memory_space=pltpu.VMEM)] * len(outs),
        scratch_shapes=[pltpu.VMEM(s, jnp.float32) for s in scratch],
        compiler_params=pltpu.CompilerParams(vmem_limit_bytes=VMEM_LIMIT),
        name=name,
    )(*args)


def pairs(first, step, size):
    devices = lax.axis_size("gz")
    return [[(b + i) % devices, (b + i + step) % devices] for b in range(0, devices, size) for i in first]


def gather(value, first, step, size):
    return lax.all_gather(value, "gz", axis_index_groups=pairs(first, step, size))


def cores(value):
    return gather(value, (0,), 1, 2)


def across(value):
    return gather(value, (1,), 1, 2)


def swap(value, step):
    devices = lax.axis_size("gz")
    ways = []
    for i in range(1, devices, 2):
        ways += [(i, (i + step) % devices), ((i + step) % devices, i)]
    return lax.ppermute(value, "gz", ways)


def row_pairs(value):
    planes, rows = lax.axis_size("gz"), lax.axis_size("gy")
    members = []
    for z in range(planes):
        for y in range(z % 2, rows, 2):
            members.append([z * rows + y, z * rows + (y + 1) % rows])
    return lax.all_gather(value, ("gz", "gy"), axis_index_groups=members)


def pick(value, index):
    return lax.dynamic_index_in_dim(value, index, 0, keepdims=False)


def local(source, conduct):
    z = lax.axis_index("gz")
    y = lax.axis_index("gy")
    core = z % 2
    prm = jnp.stack([core, y % 2, y, z]).astype(jnp.int32)
    place = (core + y) % 2
    (remain,) = call(
        prepare_kernel, [f32(4, 8, 4, 512)], [(4, 128, 128)], source, conduct, scalars=False, name="prepare"
    )
    adjoint = None
    kept = None
    for cycle in range(CYCLES):
        first, last = cycle == 0, cycle == CYCLES - 1
        parts = 2 if first else 1
        chip = cores(remain)
        flat = chip.reshape(8, *chip.shape[2:])
        halves = row_pairs(jnp.where(place == 0, flat[:, :, 2:4], flat[:, :, 0:2]))
        halves = cores(jnp.where(place == 0, halves[1], halves[0]))
        laid = call(
            functools.partial(rows_kernel, parts),
            [f32(8, 4, 8, 512), f32(6, 4, 8, 512)] * parts,
            [],
            prm,
            chip,
            halves,
            name="rows",
        )
        args = [prm]
        if first:
            side_k = swap(laid[3], 1)
        args += [laid[0], across(laid[1])]
        if first:
            args += [laid[2], side_k]
        outs = [f32(14, 4, 8, 512), f32(10, 4, 8, 512), f32(parts, 2, 2, 4, 256), f32(256, 128)]
        state = [f32(14, 4, 8, 512)] * 2
        scratch = [(14, 4, 8, 512)] * 3
        body = functools.partial(fine_down_kernel, first)
        if first:
            rhs0, field0, low, edge, cond0, inv0 = call(body, outs + state, scratch, *args, name="fine_down_first")
        else:
            cond0, inv0 = kept[0:2]
            rhs0, field0, low, edge = call(body, outs, scratch, *args, inv0, name="fine_down")
        copies = jnp.broadcast_to(low, (lax.axis_size("gy"), *low.shape))
        rows = lax.all_to_all(copies, "gy", split_axis=0, concat_axis=0, tiled=True)
        (rows,) = call(pick_kernel, [f32(5, parts, 2, 2, 4, 256)], [], prm, rows, name="pick")
        chip = cores(rows)
        far = cores(pick(across(chip), core))
        outs = [f32(12, 2, 24, 256), f32(8, 2, 24, 256), f32(parts, 2, 24, 128)]
        state = [f32(12, 2, 24, 256)] * 2
        scratch = [(12, 2, 24, 256)] * 3
        body = functools.partial(middle_down_kernel, first)
        if first:
            rhs1, field1, low, cond1, inv1 = call(
                body, outs + state, scratch, prm, chip, far, name="middle_down_first"
            )
        else:
            cond1, inv1 = kept[2:4]
            rhs1, field1, low = call(body, outs, scratch, prm, chip, far, inv1, name="middle_down")
        beside = [swap(low, 1), swap(low, 3)]
        far = cores(jnp.concatenate([edge] + [v.reshape(48 * parts, 128) for v in beside], axis=0))
        outs = [f32(8, 2, 16, 256), f32(3, 2, 16, 256)]
        state = [f32(10, 1, 24, 128)] * 2
        scratch = [(10, 1, 24, 128)] * 4
        body = functools.partial(coarse_kernel, first)
        if first:
            start, send, cond2, inv2 = call(
                body, outs + state, scratch, prm, low, far, field1, cond1, name="coarse_first"
            )
        else:
            cond2, inv2 = kept[4:6]
            start, send = call(
                body, outs, scratch, prm, low, far, field1, cond1, cond2, inv2, name="coarse"
            )
        side = across(send)
        more = cores(pick(side.reshape(6, *side.shape[2:]), 2 + core))
        outs = [f32(4, 4, 4, 512)] * 2
        scratch = [(12, 2, 16, 256)] * 3 + [(12, 4, 8, 512)] * 3
        args = [prm, start, side, more, far, rhs1, cond1, inv1, rhs0, field0, cond0, inv0]
        if last:
            args.append(adjoint)
        adjoint, remain = call(functools.partial(up_kernel, last), outs, scratch, *args, name="up")
        kept = (cond0, inv0, cond1, inv1, cond2, inv2)
    return tuple(
        call(
            finish_kernel,
            [f32(4, 16, 512)] * 2,
            [(4, 128, 128)],
            adjoint,
            remain,
            scalars=False,
            name="finish",
        )
    )


def solution(mesh):
    placed = (P("gz", "gy", None), P("gz", "gy", None))
    return jax.shard_map(local, mesh=mesh, in_specs=placed, out_specs=placed, check_vma=False)
```

```python
import functools

import jax
import jax.numpy as jnp
from jax import lax
from jax.experimental import pallas as pl
from jax.experimental.pallas import tpu as pltpu
from jax.sharding import PartitionSpec as P

DEGREE = 3
COARSE_DEGREE = 4
CYCLES = 2

CHEB_LOW = 0.3
CHEB_HIGH = 1.9
SCALES = (4.0, 1.0, 0.25)
LANES = 128
VMEM_LIMIT = 16 * 1024 * 1024


def chebyshev(steps):
    theta = (CHEB_HIGH + CHEB_LOW) / 2.0
    delta = (CHEB_HIGH - CHEB_LOW) / 2.0
    sigma = theta / delta
    rho = 1.0 / sigma
    pairs = [(0.0, 1.0 / theta)]
    for _ in range(steps - 1):
        rho_next = 1.0 / (2.0 * sigma - rho)
        pairs.append((rho_next * rho, 2.0 * rho_next / delta))
        rho = rho_next
    return pairs


def lanes(c):
    return slice(c * LANES, (c + 1) * LANES)


def load(ref, z, size):
    return [[ref[z, d, :, lanes(c)] for c in range(size)] for d in range(size)]


def load_ends(ref, z, size):
    top = ref.shape[2]
    return [
        [
            jnp.concatenate([ref[z, d, 0:8, lanes(c)], ref[z, d, top - 8 : top, lanes(c)]], axis=0)
            for c in range(size)
        ]
        for d in range(size)
    ]


def pack(ref, row, tiles):
    for d in range(2):
        for c in range(2):
            at = row + 16 * (2 * d + c)
            ref[at : at + 16, :] = tiles[d][c]


def unpack(ref, core, row):
    return [[ref[core, row + 16 * (2 * d + c) : row + 16 * (2 * d + c) + 16, :] for c in range(2)] for d in range(2)]


def store(ref, z, tiles):
    for d, line in enumerate(tiles):
        for c, tile in enumerate(line):
            ref[z, d, :, lanes(c)] = tile


def neighbours(below, here, above, size):
    rows = here[0][0].shape[0]
    lane = lax.broadcasted_iota(jnp.int32, (rows, LANES), 1)
    first, last = lane == 0, lane == LANES - 1
    out = []
    for d in range(size):
        line = []
        for c in range(size):
            if c > 0:
                left = here[d][c - 1]
            else:
                left = jnp.where(first, 0.0, pltpu.roll(here[d][size - 1], 1, 1))
            if c < size - 1:
                right = here[d][c + 1]
            else:
                right = jnp.where(last, 0.0, pltpu.roll(here[d][0], LANES - 1, 1))
            low = here[d - 1][c] if d > 0 else pltpu.roll(here[size - 1][c], 1, 0)
            high = here[d + 1][c] if d < size - 1 else pltpu.roll(here[0][c], rows - 1, 0)
            line.append(((below[d][c] + above[d][c]) + (left + right)) + (low + high))
        out.append(line)
    return out


def first_step(lo, hi, rhs, inv, w, dw, size, beta, group=1):
    def body(step, carry):
        for z in [lo + step * group + g for g in range(group)]:
            for d in range(size):
                for c in range(size):
                    value = (beta * rhs[z, d, :, lanes(c)]) * inv[z, d, :, lanes(c)]
                    w[z, d, :, lanes(c)] = value
                    dw[z, d, :, lanes(c)] = value
        return carry

    lax.fori_loop(0, (hi - lo) // group, body, 0)


def sweep(lo, hi, src, dst, dst_shift, dw, rhs, inv, shift, size, scale, alpha, beta, loader=load, group=1):
    def body(step, carry):
        start = lo + step * group
        planes = {g: load(src, start + g, size) for g in range(-1, group + 1)}
        done = []
        for g in range(group):
            z, here = start + g, planes[g]
            near = neighbours(planes[g - 1], here, planes[g + 1], size)
            f = loader(rhs, z + shift, size)
            i = loader(inv, z + shift, size)
            for d in range(size):
                for c in range(size):
                    q = i[d][c] * (f[d][c] + scale * near[d][c]) - here[d][c]
                    change = beta * q
                    if alpha != 0.0:
                        change = change + alpha * dw[z, d, :, lanes(c)]
                    done.append((z, d, c, change, here[d][c] + change))
        for z, d, c, change, value in done:
            dw[z, d, :, lanes(c)] = change
            dst[z + dst_shift, d, :, lanes(c)] = value
        return carry

    lax.fori_loop(0, (hi - lo) // group, body, 0)


def residual_plane(src, z, rhs, inv, zr, size, scale):
    here = load(src, z, size)
    near = neighbours(load(src, z - 1, size), here, load(src, z + 1, size), size)
    out = []
    for d in range(size):
        line = []
        for c in range(size):
            i = inv[zr, d, :, lanes(c)]
            line.append((rhs[zr, d, :, lanes(c)] + scale * near[d][c]) - here[d][c] / i)
        out.append(line)
    return out


def halve(one, two, size):
    half = size // 2
    return [
        [
            0.125
            * (
                ((one[2 * d][2 * c] + one[2 * d][2 * c + 1]) + (one[2 * d + 1][2 * c] + one[2 * d + 1][2 * c + 1]))
                + ((two[2 * d][2 * c] + two[2 * d][2 * c + 1]) + (two[2 * d + 1][2 * c] + two[2 * d + 1][2 * c + 1]))
            )
            for c in range(half)
        ]
        for d in range(half)
    ]


def inverse_of(cond, scale):
    return 1.0 / (1.0 / cond + 6.0 * scale)


def selector(to_tiles):
    rows = lax.broadcasted_iota(jnp.int32, (512, 512), 0)
    cols = lax.broadcasted_iota(jnp.int32, (512, 512), 1)
    if to_tiles:
        hit = rows == 4 * (cols % LANES) + cols // LANES
    else:
        hit = cols == 4 * (rows % LANES) + rows // LANES
    return jnp.where(hit, 1.0, 0.0).astype(jnp.float32)


def reorder(rows, to_tiles):
    return jnp.dot(
        rows, selector(to_tiles), precision=lax.Precision.HIGHEST, preferred_element_type=jnp.float32
    )


def prepare_kernel(source, cond, out, work):
    rows = jnp.concatenate([source[...].reshape(64, 512), cond[...].reshape(64, 512)], axis=0)
    tiles = reorder(rows, True)
    for c in range(4):
        work[c] = tiles[:, lanes(c)]
    for a in range(2):
        for z in range(4):
            for d in range(4):
                for c in range(4):
                    out[z, 4 * a + d, :, lanes(c)] = work[c, pl.ds(64 * a + 16 * z + d, 4, stride=4), :]


def finish_kernel(adjoint, remain, out_a, out_r, work):
    for a, ref in enumerate((adjoint, remain)):
        for z in range(4):
            for d in range(4):
                for c in range(4):
                    work[c, pl.ds(64 * a + 16 * z + d, 4, stride=4), :] = ref[z, d, :, lanes(c)]
    rows = reorder(jnp.concatenate([work[c] for c in range(4)], axis=1), False)
    out_a[...] = rows[0:64].reshape(4, 16, 512)
    out_r[...] = rows[64:128].reshape(4, 16, 512)


def rows_kernel(parts, prm, chip, halves, *outs):
    core, odd = prm[0], prm[1]
    for a in range(parts):
        whole, send = outs[2 * a : 2 * a + 2]
        for t in range(8):
            for d in range(4):
                whole[t, d, 0:4, :] = chip[t // 4, t % 4, 4 * a + d]
                whole[t, d, 4:6, :] = halves[odd, t, 4 * a + d]
                whole[t, d, 6:8, :] = halves[1 - odd, t, 4 * a + d]
        for t in range(6):
            send[t] = whole[2 * core + t]


def fine_down_kernel(first, prm, *refs):
    if first:
        whole, side, whole_k, side_k, rhs, field, low, edge, cond, inv, wa, wb, dw = refs
    else:
        whole, side, inv, rhs, field, low, edge, wa, wb, dw = refs
    core = prm[0]

    @pl.when(core == 0)
    def _():
        for t in range(6):
            rhs[t] = side[0, t]
            if first:
                cond[t] = side_k[t]
        for t in range(8):
            rhs[6 + t] = whole[t]
            if first:
                cond[6 + t] = whole_k[t]

    @pl.when(core == 1)
    def _():
        for t in range(8):
            rhs[t] = whole[t]
            if first:
                cond[t] = whole_k[t]
        for t in range(6):
            rhs[8 + t] = side[1, t]
            if first:
                cond[8 + t] = side_k[t]

    if first:

        def fill(t, carry):
            inv[t] = inverse_of(cond[t], SCALES[0])
            return carry

        lax.fori_loop(0, 14, fill, 0)
    steps = chebyshev(DEGREE)
    first_step(0, 14, rhs, inv, wa, dw, 4, steps[0][1])
    sweep(1, 13, wa, wb, 0, dw, rhs, inv, 0, 4, SCALES[0], *steps[1])
    sweep(2, 12, wb, field, -2, dw, rhs, inv, 0, 4, SCALES[0], *steps[2])
    for q in range(2):
        for d in range(4):
            for c in range(4):
                row = 8 * ((q * 4 + d) * 4 + c)
                edge[row : row + 8, :] = field[4 + q, d, :, lanes(c)]
    for t in range(2):
        z = 6 - 2 * core + 2 * t
        one = residual_plane(field, z - 2, rhs, inv, z, 4, SCALES[0])
        two = residual_plane(field, z - 1, rhs, inv, z + 1, 4, SCALES[0])
        mean = halve(one, two, 4)
        for d in range(2):
            for c in range(2):
                for r in range(8):
                    low[r, 0, t, d, :, lanes(c)] = mean[d][c][0:4]
        if first:
            mean = halve(load(cond, z, 4), load(cond, z + 1, 4), 4)
            for d in range(2):
                for c in range(2):
                    for r in range(8):
                        low[r, 1, t, d, :, lanes(c)] = mean[d][c][0:4]


def pick_kernel(prm, rows, out):
    for j, step in enumerate((0, 1, 2, 6, 7)):
        out[j] = rows[lax.rem(prm[2] + step, 8)]


def middle_down_kernel(first, prm, chip, far, *refs):
    if first:
        rhs, field, low, near, cond, inv, wa, wb, dw = refs
    else:
        inv, rhs, field, low, near, wa, wb, dw = refs
    core = prm[0]
    for t in range(12):
        if t < 4:
            ref, at = far.at[0], t
        elif t < 8:
            ref, at = chip, t - 4
        else:
            ref, at = far.at[1], t - 8
        for d in range(2):
            for j, row in enumerate((0, 4, 8, 16, 20)):
                rhs[t, d, row : row + 4, :] = ref[at // 2, j, 0, at % 2, d]
                if first:
                    cond[t, d, row : row + 4, :] = ref[at // 2, j, 1, at % 2, d]
            rhs[t, d, 12:16, :] = jnp.zeros((4, 256), jnp.float32)
            if first:
                cond[t, d, 12:16, :] = jnp.ones((4, 256), jnp.float32)
    if first:

        def fill(t, carry):
            inv[t] = inverse_of(cond[t], SCALES[1])
            return carry

        lax.fori_loop(0, 12, fill, 0)
    steps = chebyshev(DEGREE)
    first_step(0, 12, rhs, inv, wa, dw, 2, steps[0][1], group=2)
    sweep(1, 11, wa, wb, 0, dw, rhs, inv, 0, 2, SCALES[1], *steps[1], group=2)
    sweep(2, 10, wb, field, -2, dw, rhs, inv, 0, 2, SCALES[1], *steps[2], group=2)
    for h in range(2):
        z = 4 + 2 * h
        one = residual_plane(field, z - 2, rhs, inv, z, 2, SCALES[1])
        two = residual_plane(field, z - 1, rhs, inv, z + 1, 2, SCALES[1])
        low[0, h] = halve(one, two, 2)[0][0]
        if first:
            low[1, h] = halve(load(cond, z, 2), load(cond, z + 1, 2), 2)[0][0]
    for t in range(3):
        pack(near, 64 * t, load_ends(field, 4 - 3 * core + t, 2))
    at = 192
    if first:
        pack(near, at, load_ends(cond, 8 - 5 * core, 2))
        at += 64
    for a in range(2 if first else 1):
        for h in range(2):
            row = at + 48 * a + 24 * h
            near[row : row + 24, :] = low[a, h]


def up_kernel(first, prm, low, far, middle, mid_rhs, mid_cond, mid_inv, fine, rhs, cond, inv, *refs):
    if first:
        adjoint, remain, ends, low_cond, low_inv = refs[:5]
    else:
        ends, low_cond, low_inv, before, adjoint, remain = refs[:6]
    low_rhs, la, lb, ldw, start, mid_a, mid_b, mid_dw, wa, wb, dw = refs[-11:]
    core = prm[0]
    parts = 2 if first else 1
    base = 256 + 192 + (64 if first else 0)

    for a in range(parts):
        for t in range(14):
            if t < 6:
                row = base + 48 * parts * (2 - t // 2) + 48 * a + 24 * (t % 2)
                value = far[0, row : row + 24, :]
            elif t < 8:
                value = low[a, t - 6]
            else:
                row = base + 48 * parts * (t // 2 - 4) + 48 * a + 24 * (t % 2)
                value = far[1, row : row + 24, :]
            if a == 0:
                low_rhs[t, 0] = value
            else:
                low_cond[t, 0] = value
                low_inv[t, 0] = inverse_of(value, SCALES[2])
    steps = chebyshev(COARSE_DEGREE)
    first_step(0, 14, low_rhs, low_inv, la, ldw, 1, steps[0][1], group=14)
    sweep(1, 13, la, lb, 0, ldw, low_rhs, low_inv, 0, 1, SCALES[2], *steps[1], group=6)
    sweep(2, 12, lb, la, 0, ldw, low_rhs, low_inv, 0, 1, SCALES[2], *steps[2], group=5)
    sweep(3, 11, la, lb, 0, ldw, low_rhs, low_inv, 0, 1, SCALES[2], *steps[3], group=4)

    for t in range(3):
        store(start, t, unpack(far, 0, 256 + 64 * t))
        store(start, 11 + t, unpack(far, 1, 256 + 64 * t))
    for t in range(8):
        store(start, 3 + t, load_ends(middle, t, 2))
    if first:
        store(ends, 0, unpack(far, 0, 448))
        store(ends, 13, unpack(far, 1, 448))
        for t in range(12):
            store(ends, 1 + t, load_ends(mid_cond, t, 2))
    for t in range(12):
        at = (t + 1) // 2 + 3 + core
        value = lb[at, 0] / low_cond[at, 0]
        value = jnp.concatenate([value[0:8], value[16:24]], axis=0)
        here = load(start, t + 2 * core, 2)
        k = load(ends, t + 2 * core, 2)
        store(mid_a, t, [[here[d][c] + k[d][c] * value for c in range(2)] for d in range(2)])

    def beyond(other, at):
        for q in range(2):
            for d in range(4):
                for c in range(4):
                    row = 8 * ((q * 4 + d) * 4 + c)
                    wa[at + q, d, :, lanes(c)] = far[other, row : row + 8, :]

    @pl.when(core == 0)
    def _():
        for t in range(10):
            wa[t] = fine[t]
        beyond(1, 10)

    @pl.when(core == 1)
    def _():
        for t in range(10):
            wa[2 + t] = fine[t]
        beyond(0, 0)

    steps = chebyshev(DEGREE)
    shift = 2 * core - 1
    sweep(1, 11, mid_a, mid_b, 0, mid_dw, mid_rhs, mid_inv, shift, 2, SCALES[1], *steps[0], loader=load_ends, group=2)
    sweep(2, 10, mid_b, mid_a, 0, mid_dw, mid_rhs, mid_inv, shift, 2, SCALES[1], *steps[1], loader=load_ends, group=2)
    sweep(3, 9, mid_a, mid_b, 0, mid_dw, mid_rhs, mid_inv, shift, 2, SCALES[1], *steps[2], loader=load_ends, group=2)

    near = lax.broadcasted_iota(jnp.int32, (8, LANES), 0) < 6
    ahead = 2 - 2 * core

    def correct(t, carry):
        k = load(ends, t + 2 * core, 2)
        for d in range(2):
            for c in range(2):
                value = mid_b[t, d, :, lanes(c)] / k[d][c]
                value = jnp.where(near, value[0:8], value[8:16])
                for z in range(2):
                    v = 2 * (t - 3) + z
                    for dd in (2 * d, 2 * d + 1):
                        for cc in (2 * c, 2 * c + 1):
                            wa[v, dd, :, lanes(cc)] = (
                                wa[v, dd, :, lanes(cc)] + cond[v + ahead, dd, :, lanes(cc)] * value
                            )
        return carry

    lax.fori_loop(3, 9, correct, 0)
    sweep(1, 11, wa, wb, 0, dw, rhs, inv, ahead, 4, SCALES[0], *steps[0])
    sweep(2, 10, wb, wa, 0, dw, rhs, inv, ahead, 4, SCALES[0], *steps[1])
    sweep(3, 9, wa, wb, 0, dw, rhs, inv, ahead, 4, SCALES[0], *steps[2])

    def finish(t, carry):
        left = residual_plane(wb, t + 4, rhs, inv, t + 4 + ahead, 4, SCALES[0])
        for d in range(4):
            for c in range(4):
                value = wb[t + 4, d, :, lanes(c)] / cond[t + 4 + ahead, d, :, lanes(c)]
                value = value[0:4]
                if not first:
                    value = value + before[t, d, :, lanes(c)]
                adjoint[t, d, :, lanes(c)] = value
                remain[t, d, :, lanes(c)] = left[d][c][0:4]
        return carry

    lax.fori_loop(0, 4, finish, 0)


def f32(*shape):
    return jax.ShapeDtypeStruct(shape, jnp.float32)


def call(body, outs, scratch, *args, scalars=True, name=None):
    specs = [pl.BlockSpec(memory_space=pltpu.VMEM) if scalars else pl.BlockSpec()] * len(args)
    if scalars:
        specs[0] = pl.BlockSpec(memory_space=pltpu.SMEM)
    return pl.pallas_call(
        body,
        out_shape=outs,
        in_specs=specs,
        out_specs=[pl.BlockSpec(memory_space=pltpu.VMEM)] * len(outs),
        scratch_shapes=[pltpu.VMEM(s, jnp.float32) for s in scratch],
        compiler_params=pltpu.CompilerParams(vmem_limit_bytes=VMEM_LIMIT),
        name=name,
    )(*args)


def pairs(first, step, size):
    devices = lax.axis_size("gz")
    return [[(b + i) % devices, (b + i + step) % devices] for b in range(0, devices, size) for i in first]


def gather(value, first, step, size):
    return lax.all_gather(value, "gz", axis_index_groups=pairs(first, step, size))


def cores(value):
    return gather(value, (0,), 1, 2)


def across(value):
    return gather(value, (1,), 1, 2)


def swap(value, step):
    devices = lax.axis_size("gz")
    ways = []
    for i in range(1, devices, 2):
        ways += [(i, (i + step) % devices), ((i + step) % devices, i)]
    return lax.ppermute(value, "gz", ways)


def row_pairs(value):
    planes, rows = lax.axis_size("gz"), lax.axis_size("gy")
    members = []
    for z in range(planes):
        for y in range(z % 2, rows, 2):
            members.append([z * rows + y, z * rows + (y + 1) % rows])
    return lax.all_gather(value, ("gz", "gy"), axis_index_groups=members)


def pick(value, index):
    return lax.dynamic_index_in_dim(value, index, 0, keepdims=False)


def local(source, conduct):
    z = lax.axis_index("gz")
    y = lax.axis_index("gy")
    core = z % 2
    prm = jnp.stack([core, y % 2, y, z]).astype(jnp.int32)
    place = (core + y) % 2
    (remain,) = call(
        prepare_kernel, [f32(4, 8, 4, 512)], [(4, 128, 128)], source, conduct, scalars=False, name="prepare"
    )
    adjoint = None
    kept = None
    for cycle in range(CYCLES):
        first = cycle == 0
        parts = 2 if first else 1
        chip = cores(remain)
        flat = chip.reshape(8, *chip.shape[2:])
        halves = row_pairs(jnp.where(place == 0, flat[:, :, 2:4], flat[:, :, 0:2]))
        halves = cores(jnp.where(place == 0, halves[1], halves[0]))
        laid = call(
            functools.partial(rows_kernel, parts),
            [f32(8, 4, 8, 512), f32(6, 4, 8, 512)] * parts,
            [],
            prm,
            chip,
            halves,
            name="rows",
        )
        args = [prm]
        if first:
            side_k = swap(laid[3], 1)
        args += [laid[0], across(laid[1])]
        if first:
            args += [laid[2], side_k]
        outs = [f32(14, 4, 8, 512), f32(10, 4, 8, 512), f32(8, parts, 2, 2, 4, 256), f32(256, 128)]
        state = [f32(14, 4, 8, 512)] * 2
        scratch = [(14, 4, 8, 512)] * 3
        body = functools.partial(fine_down_kernel, first)
        if first:
            rhs0, field0, low, edge, cond0, inv0 = call(body, outs + state, scratch, *args, name="fine_down_first")
        else:
            cond0, inv0 = kept[0:2]
            rhs0, field0, low, edge = call(body, outs, scratch, *args, inv0, name="fine_down")
        rows = lax.all_to_all(low, "gy", split_axis=0, concat_axis=0, tiled=True)
        (rows,) = call(pick_kernel, [f32(5, parts, 2, 2, 4, 256)], [], prm, rows, name="pick")
        chip = cores(rows)
        far = cores(pick(across(chip), core))
        near_rows = 192 + (64 if first else 0) + 48 * parts
        outs = [f32(12, 2, 24, 256), f32(8, 2, 24, 256), f32(parts, 2, 24, 128), f32(near_rows, 128)]
        state = [f32(12, 2, 24, 256)] * 2
        scratch = [(12, 2, 24, 256)] * 3
        body = functools.partial(middle_down_kernel, first)
        if first:
            rhs1, field1, low, near, cond1, inv1 = call(
                body, outs + state, scratch, prm, chip, far, name="middle_down_first"
            )
        else:
            cond1, inv1 = kept[2:4]
            rhs1, field1, low, near = call(body, outs, scratch, prm, chip, far, inv1, name="middle_down")
        flat = low.reshape(48 * parts, 128)
        beside = [swap(near, 1), swap(flat, 3), swap(flat, 5)]
        far = cores(jnp.concatenate([edge, *beside], axis=0))
        outs = [f32(4, 4, 4, 512)] * 2
        scratch = [(14, 1, 24, 128)] * 4 + [(14, 2, 16, 256)] + [(12, 2, 16, 256)] * 3 + [(12, 4, 8, 512)] * 3
        args = [prm, low, far, field1, rhs1, cond1, inv1, field0, rhs0, cond0, inv0]
        body = functools.partial(up_kernel, first)
        if first:
            state = [f32(14, 2, 16, 256), f32(14, 1, 24, 128), f32(14, 1, 24, 128)]
            adjoint, remain, *coarse = call(body, outs + state, scratch, *args, name="up_first")
            kept = (cond0, inv0, cond1, inv1, *coarse)
        else:
            adjoint, remain = call(body, outs, scratch, *args, *kept[4:7], adjoint, name="up")
    return tuple(
        call(
            finish_kernel,
            [f32(4, 16, 512)] * 2,
            [(4, 128, 128)],
            adjoint,
            remain,
            scalars=False,
            name="finish",
        )
    )


def solution(mesh):
    placed = (P("gz", "gy", None), P("gz", "gy", None))
    return jax.shard_map(local, mesh=mesh, in_specs=placed, out_specs=placed, check_vma=False)
```

```python
import functools

import jax
import jax.numpy as jnp
from jax import lax
from jax.experimental import pallas as pl
from jax.experimental.pallas import tpu as pltpu
from jax.sharding import PartitionSpec as P

DEGREE = 3
COARSE_DEGREE = 4
CYCLES = 2

CHEB_LOW = 0.3
CHEB_HIGH = 1.9
SCALES = (4.0, 1.0, 0.25)
LANES = 128
VMEM_LIMIT = 16 * 1024 * 1024


def chebyshev(steps):
    theta = (CHEB_HIGH + CHEB_LOW) / 2.0
    delta = (CHEB_HIGH - CHEB_LOW) / 2.0
    sigma = theta / delta
    rho = 1.0 / sigma
    pairs = [(0.0, 1.0 / theta)]
    for _ in range(steps - 1):
        rho_next = 1.0 / (2.0 * sigma - rho)
        pairs.append((rho_next * rho, 2.0 * rho_next / delta))
        rho = rho_next
    return pairs


def lanes(c):
    return slice(c * LANES, (c + 1) * LANES)


def load(ref, z, size):
    return [[ref[z, d, :, lanes(c)] for c in range(size)] for d in range(size)]


def load_ends(ref, z, size):
    top = ref.shape[2]
    return [
        [
            jnp.concatenate([ref[z, d, 0:8, lanes(c)], ref[z, d, top - 8 : top, lanes(c)]], axis=0)
            for c in range(size)
        ]
        for d in range(size)
    ]


def pack(ref, row, tiles):
    for d in range(2):
        for c in range(2):
            at = row + 16 * (2 * d + c)
            ref[at : at + 16, :] = tiles[d][c]


def unpack(ref, core, row):
    return [[ref[core, row + 16 * (2 * d + c) : row + 16 * (2 * d + c) + 16, :] for c in range(2)] for d in range(2)]


def store(ref, z, tiles):
    for d, line in enumerate(tiles):
        for c, tile in enumerate(line):
            ref[z, d, :, lanes(c)] = tile


def neighbours(below, here, above, size):
    rows = here[0][0].shape[0]
    lane = lax.broadcasted_iota(jnp.int32, (rows, LANES), 1)
    first, last = lane == 0, lane == LANES - 1
    out = []
    for d in range(size):
        line = []
        for c in range(size):
            if c > 0:
                left = here[d][c - 1]
            else:
                left = jnp.where(first, 0.0, pltpu.roll(here[d][size - 1], 1, 1))
            if c < size - 1:
                right = here[d][c + 1]
            else:
                right = jnp.where(last, 0.0, pltpu.roll(here[d][0], LANES - 1, 1))
            low = here[d - 1][c] if d > 0 else pltpu.roll(here[size - 1][c], 1, 0)
            high = here[d + 1][c] if d < size - 1 else pltpu.roll(here[0][c], rows - 1, 0)
            line.append(((below[d][c] + above[d][c]) + (left + right)) + (low + high))
        out.append(line)
    return out


def first_step(lo, hi, rhs, inv, w, dw, size, beta):
    for z in range(lo, hi):
        for d in range(size):
            for c in range(size):
                value = (beta * rhs[z, d, :, lanes(c)]) * inv[z, d, :, lanes(c)]
                w[z, d, :, lanes(c)] = value
                dw[z, d, :, lanes(c)] = value


def sweep(lo, hi, src, dst, dst_shift, dw, rhs, inv, shift, size, scale, alpha, beta, loader=load):
    planes = {z: load(src, z, size) for z in range(lo - 1, hi + 1)}
    for z in range(lo, hi):
        here = planes[z]
        near = neighbours(planes[z - 1], here, planes[z + 1], size)
        f = loader(rhs, z + shift, size)
        i = loader(inv, z + shift, size)
        for d in range(size):
            for c in range(size):
                q = i[d][c] * (f[d][c] + scale * near[d][c]) - here[d][c]
                change = beta * q
                if alpha != 0.0:
                    change = change + alpha * dw[z, d, :, lanes(c)]
                dw[z, d, :, lanes(c)] = change
                dst[z + dst_shift, d, :, lanes(c)] = here[d][c] + change


def residual_plane(src, z, rhs, inv, zr, size, scale):
    here = load(src, z, size)
    near = neighbours(load(src, z - 1, size), here, load(src, z + 1, size), size)
    out = []
    for d in range(size):
        line = []
        for c in range(size):
            i = inv[zr, d, :, lanes(c)]
            line.append((rhs[zr, d, :, lanes(c)] + scale * near[d][c]) - here[d][c] / i)
        out.append(line)
    return out


def halve(one, two, size):
    half = size // 2
    return [
        [
            0.125
            * (
                ((one[2 * d][2 * c] + one[2 * d][2 * c + 1]) + (one[2 * d + 1][2 * c] + one[2 * d + 1][2 * c + 1]))
                + ((two[2 * d][2 * c] + two[2 * d][2 * c + 1]) + (two[2 * d + 1][2 * c] + two[2 * d + 1][2 * c + 1]))
            )
            for c in range(half)
        ]
        for d in range(half)
    ]


def inverse_of(cond, scale):
    return 1.0 / (1.0 / cond + 6.0 * scale)


def selector(to_tiles):
    rows = lax.broadcasted_iota(jnp.int32, (512, 512), 0)
    cols = lax.broadcasted_iota(jnp.int32, (512, 512), 1)
    if to_tiles:
        hit = rows == 4 * (cols % LANES) + cols // LANES
    else:
        hit = cols == 4 * (rows % LANES) + rows // LANES
    return jnp.where(hit, 1.0, 0.0).astype(jnp.float32)


def reorder(rows, to_tiles):
    return jnp.dot(
        rows, selector(to_tiles), precision=lax.Precision.HIGHEST, preferred_element_type=jnp.float32
    )


def prepare_kernel(source, cond, out, both, work, sems):
    copies = [pltpu.make_async_copy(ref, both.at[a], sems.at[a]) for a, ref in enumerate((source, cond))]
    for copy in copies:
        copy.start()
    for copy in copies:
        copy.wait()
    tiles = reorder(both[...].reshape(128, 512), True)
    for c in range(4):
        work[c] = tiles[:, lanes(c)]
    for a in range(2):
        for z in range(4):
            for d in range(4):
                for c in range(4):
                    out[z, 4 * a + d, :, lanes(c)] = work[c, pl.ds(64 * a + 16 * z + d, 4, stride=4), :]


def finish_kernel(adjoint, remain, out_a, out_r, work):
    for a, ref in enumerate((adjoint, remain)):
        for z in range(4):
            for d in range(4):
                for c in range(4):
                    work[c, pl.ds(64 * a + 16 * z + d, 4, stride=4), :] = ref[z, d, :, lanes(c)]
    rows = reorder(jnp.concatenate([work[c] for c in range(4)], axis=1), False)
    out_a[...] = rows[0:64].reshape(4, 16, 512)
    out_r[...] = rows[64:128].reshape(4, 16, 512)


def rows_kernel(parts, prm, chip, halves, *outs):
    core, odd = prm[0], prm[1]
    for a in range(parts):
        whole, send = outs[2 * a : 2 * a + 2]
        for t in range(8):
            for d in range(4):
                whole[t, d, 0:4, :] = chip[t // 4, t % 4, 4 * a + d]
                whole[t, d, 4:6, :] = halves[odd, t, 4 * a + d]
                whole[t, d, 6:8, :] = halves[1 - odd, t, 4 * a + d]
        for t in range(6):
            send[t] = whole[2 * core + t]


def fine_down_kernel(first, prm, *refs):
    if first:
        whole, side, whole_k, side_k, rhs, field, low, edge, cond, inv, wa, wb, dw = refs
    else:
        whole, side, inv, rhs, field, low, edge, wa, wb, dw = refs
    core = prm[0]

    @pl.when(core == 0)
    def _():
        for t in range(6):
            rhs[t] = side[0, t]
            if first:
                cond[t] = side_k[t]
        for t in range(8):
            rhs[6 + t] = whole[t]
            if first:
                cond[6 + t] = whole_k[t]

    @pl.when(core == 1)
    def _():
        for t in range(8):
            rhs[t] = whole[t]
            if first:
                cond[t] = whole_k[t]
        for t in range(6):
            rhs[8 + t] = side[1, t]
            if first:
                cond[8 + t] = side_k[t]

    if first:
        for t in range(14):
            inv[t] = inverse_of(cond[t], SCALES[0])
    steps = chebyshev(DEGREE)
    first_step(0, 14, rhs, inv, wa, dw, 4, steps[0][1])
    sweep(1, 13, wa, wb, 0, dw, rhs, inv, 0, 4, SCALES[0], *steps[1])
    sweep(2, 12, wb, field, -2, dw, rhs, inv, 0, 4, SCALES[0], *steps[2])
    for q in range(2):
        for d in range(4):
            for c in range(4):
                row = 8 * ((q * 4 + d) * 4 + c)
                edge[row : row + 8, :] = field[4 + q, d, :, lanes(c)]
    for t in range(2):
        z = 6 - 2 * core + 2 * t
        one = residual_plane(field, z - 2, rhs, inv, z, 4, SCALES[0])
        two = residual_plane(field, z - 1, rhs, inv, z + 1, 4, SCALES[0])
        mean = halve(one, two, 4)
        for d in range(2):
            for c in range(2):
                for r in range(8):
                    low[r, 0, t, d, :, lanes(c)] = mean[d][c][0:4]
        if first:
            mean = halve(load(cond, z, 4), load(cond, z + 1, 4), 4)
            for d in range(2):
                for c in range(2):
                    for r in range(8):
                        low[r, 1, t, d, :, lanes(c)] = mean[d][c][0:4]


def pick_kernel(prm, rows, out):
    for j, step in enumerate((0, 1, 2, 6, 7)):
        out[j] = rows[lax.rem(prm[2] + step, 8)]


def middle_down_kernel(first, prm, chip, far, *refs):
    if first:
        rhs, field, low, near, cond, inv, wa, wb, dw = refs
    else:
        inv, rhs, field, low, near, wa, wb, dw = refs
    core = prm[0]
    for t in range(12):
        if t < 4:
            ref, at = far.at[0], t
        elif t < 8:
            ref, at = chip, t - 4
        else:
            ref, at = far.at[1], t - 8
        for d in range(2):
            for j, row in enumerate((0, 4, 8, 16, 20)):
                rhs[t, d, row : row + 4, :] = ref[at // 2, j, 0, at % 2, d]
                if first:
                    cond[t, d, row : row + 4, :] = ref[at // 2, j, 1, at % 2, d]
            rhs[t, d, 12:16, :] = jnp.zeros((4, 256), jnp.float32)
            if first:
                cond[t, d, 12:16, :] = jnp.ones((4, 256), jnp.float32)
    if first:
        for t in range(12):
            inv[t] = inverse_of(cond[t], SCALES[1])
    steps = chebyshev(DEGREE)
    first_step(0, 12, rhs, inv, wa, dw, 2, steps[0][1])
    sweep(1, 11, wa, wb, 0, dw, rhs, inv, 0, 2, SCALES[1], *steps[1])
    sweep(2, 10, wb, field, -2, dw, rhs, inv, 0, 2, SCALES[1], *steps[2])
    for h in range(2):
        z = 4 + 2 * h
        one = residual_plane(field, z - 2, rhs, inv, z, 2, SCALES[1])
        two = residual_plane(field, z - 1, rhs, inv, z + 1, 2, SCALES[1])
        low[0, h] = halve(one, two, 2)[0][0]
        if first:
            low[1, h] = halve(load(cond, z, 2), load(cond, z + 1, 2), 2)[0][0]
    for t in range(3):
        pack(near, 64 * t, load_ends(field, 4 - 3 * core + t, 2))
    at = 192
    if first:
        pack(near, at, load_ends(cond, 8 - 5 * core, 2))
        at += 64
    for a in range(2 if first else 1):
        for h in range(2):
            row = at + 48 * a + 24 * h
            near[row : row + 24, :] = low[a, h]


def up_kernel(first, prm, low, far, middle, mid_rhs, mid_cond, mid_inv, fine, rhs, cond, inv, *refs):
    if first:
        adjoint, remain, ends, low_cond, low_inv = refs[:5]
    else:
        ends, low_cond, low_inv, before, adjoint, remain = refs[:6]
    low_rhs, la, lb, ldw, start, mid_a, mid_b, mid_dw, wa, wb, dw = refs[-11:]
    core = prm[0]
    parts = 2 if first else 1
    base = 256 + 192 + (64 if first else 0)

    for a in range(parts):
        for t in range(14):
            if t < 6:
                row = base + 48 * parts * (2 - t // 2) + 48 * a + 24 * (t % 2)
                value = far[0, row : row + 24, :]
            elif t < 8:
                value = low[a, t - 6]
            else:
                row = base + 48 * parts * (t // 2 - 4) + 48 * a + 24 * (t % 2)
                value = far[1, row : row + 24, :]
            if a == 0:
                low_rhs[t, 0] = value
            else:
                low_cond[t, 0] = value
                low_inv[t, 0] = inverse_of(value, SCALES[2])
    steps = chebyshev(COARSE_DEGREE)
    first_step(0, 14, low_rhs, low_inv, la, ldw, 1, steps[0][1])
    sweep(1, 13, la, lb, 0, ldw, low_rhs, low_inv, 0, 1, SCALES[2], *steps[1])
    sweep(2, 12, lb, la, 0, ldw, low_rhs, low_inv, 0, 1, SCALES[2], *steps[2])
    sweep(3, 11, la, lb, 0, ldw, low_rhs, low_inv, 0, 1, SCALES[2], *steps[3])

    for t in range(3):
        store(start, t, unpack(far, 0, 256 + 64 * t))
        store(start, 11 + t, unpack(far, 1, 256 + 64 * t))
    for t in range(8):
        store(start, 3 + t, load_ends(middle, t, 2))
    if first:
        store(ends, 0, unpack(far, 0, 448))
        store(ends, 13, unpack(far, 1, 448))
        for t in range(12):
            store(ends, 1 + t, load_ends(mid_cond, t, 2))
    for t in range(12):
        at = (t + 1) // 2 + 3 + core
        value = lb[at, 0] / low_cond[at, 0]
        value = jnp.concatenate([value[0:8], value[16:24]], axis=0)
        here = load(start, t + 2 * core, 2)
        k = load(ends, t + 2 * core, 2)
        store(mid_a, t, [[here[d][c] + k[d][c] * value for c in range(2)] for d in range(2)])

    def beyond(other, at):
        for q in range(2):
            for d in range(4):
                for c in range(4):
                    row = 8 * ((q * 4 + d) * 4 + c)
                    wa[at + q, d, :, lanes(c)] = far[other, row : row + 8, :]

    @pl.when(core == 0)
    def _():
        for t in range(10):
            wa[t] = fine[t]
        beyond(1, 10)

    @pl.when(core == 1)
    def _():
        for t in range(10):
            wa[2 + t] = fine[t]
        beyond(0, 0)

    steps = chebyshev(DEGREE)
    shift = 2 * core - 1
    sweep(1, 11, mid_a, mid_b, 0, mid_dw, mid_rhs, mid_inv, shift, 2, SCALES[1], *steps[0], loader=load_ends)
    sweep(2, 10, mid_b, mid_a, 0, mid_dw, mid_rhs, mid_inv, shift, 2, SCALES[1], *steps[1], loader=load_ends)
    sweep(3, 9, mid_a, mid_b, 0, mid_dw, mid_rhs, mid_inv, shift, 2, SCALES[1], *steps[2], loader=load_ends)

    near = lax.broadcasted_iota(jnp.int32, (8, LANES), 0) < 6
    ahead = 2 - 2 * core

    for t in range(3, 9):
        k = load(ends, t + 2 * core, 2)
        for d in range(2):
            for c in range(2):
                value = mid_b[t, d, :, lanes(c)] / k[d][c]
                value = jnp.where(near, value[0:8], value[8:16])
                for z in range(2):
                    v = 2 * (t - 3) + z
                    for dd in (2 * d, 2 * d + 1):
                        for cc in (2 * c, 2 * c + 1):
                            wa[v, dd, :, lanes(cc)] = (
                                wa[v, dd, :, lanes(cc)] + cond[v + ahead, dd, :, lanes(cc)] * value
                            )

    sweep(1, 11, wa, wb, 0, dw, rhs, inv, ahead, 4, SCALES[0], *steps[0])
    sweep(2, 10, wb, wa, 0, dw, rhs, inv, ahead, 4, SCALES[0], *steps[1])
    sweep(3, 9, wa, wb, 0, dw, rhs, inv, ahead, 4, SCALES[0], *steps[2])

    for t in range(4):
        left = residual_plane(wb, t + 4, rhs, inv, t + 4 + ahead, 4, SCALES[0])
        for d in range(4):
            for c in range(4):
                value = wb[t + 4, d, :, lanes(c)] / cond[t + 4 + ahead, d, :, lanes(c)]
                value = value[0:4]
                if not first:
                    value = value + before[t, d, :, lanes(c)]
                adjoint[t, d, :, lanes(c)] = value
                remain[t, d, :, lanes(c)] = left[d][c][0:4]


def f32(*shape):
    return jax.ShapeDtypeStruct(shape, jnp.float32)


def call(body, outs, scratch, *args, scalars=True, space=pltpu.VMEM, sems=0, name=None):
    specs = [pl.BlockSpec(memory_space=space)] * len(args)
    if scalars:
        specs[0] = pl.BlockSpec(memory_space=pltpu.SMEM)
    return pl.pallas_call(
        body,
        out_shape=outs,
        in_specs=specs,
        out_specs=[pl.BlockSpec(memory_space=pltpu.VMEM)] * len(outs),
        scratch_shapes=[pltpu.VMEM(s, jnp.float32) for s in scratch]
        + ([pltpu.SemaphoreType.DMA((sems,))] if sems else []),
        compiler_params=pltpu.CompilerParams(vmem_limit_bytes=VMEM_LIMIT),
        name=name,
    )(*args)


def pairs(first, step, size):
    devices = lax.axis_size("gz")
    return [[(b + i) % devices, (b + i + step) % devices] for b in range(0, devices, size) for i in first]


def gather(value, first, step, size):
    return lax.all_gather(value, "gz", axis_index_groups=pairs(first, step, size))


def cores(value):
    return gather(value, (0,), 1, 2)


def across(value):
    return gather(value, (1,), 1, 2)


def swap(value, step):
    devices = lax.axis_size("gz")
    ways = []
    for i in range(1, devices, 2):
        ways += [(i, (i + step) % devices), ((i + step) % devices, i)]
    return lax.ppermute(value, "gz", ways)


def row_pairs(value):
    planes, rows = lax.axis_size("gz"), lax.axis_size("gy")
    members = []
    for z in range(planes):
        for y in range(z % 2, rows, 2):
            members.append([z * rows + y, z * rows + (y + 1) % rows])
    return lax.all_gather(value, ("gz", "gy"), axis_index_groups=members)


def pick(value, index):
    return lax.dynamic_index_in_dim(value, index, 0, keepdims=False)


def local(source, conduct):
    z = lax.axis_index("gz")
    y = lax.axis_index("gy")
    core = z % 2
    prm = jnp.stack([core, y % 2, y, z]).astype(jnp.int32)
    place = (core + y) % 2
    (remain,) = call(
        prepare_kernel,
        [f32(4, 8, 4, 512)],
        [(2, 4, 16, 512), (4, 128, 128)],
        source,
        conduct,
        scalars=False,
        space=pl.ANY,
        sems=2,
        name="prepare",
    )
    adjoint = None
    kept = None
    for cycle in range(CYCLES):
        first = cycle == 0
        parts = 2 if first else 1
        chip = cores(remain)
        flat = chip.reshape(8, *chip.shape[2:])
        halves = row_pairs(jnp.where(place == 0, flat[:, :, 2:4], flat[:, :, 0:2]))
        halves = cores(jnp.where(place == 0, halves[1], halves[0]))
        laid = call(
            functools.partial(rows_kernel, parts),
            [f32(8, 4, 8, 512), f32(6, 4, 8, 512)] * parts,
            [],
            prm,
            chip,
            halves,
            name="rows",
        )
        args = [prm]
        if first:
            side_k = swap(laid[3], 1)
        args += [laid[0], across(laid[1])]
        if first:
            args += [laid[2], side_k]
        outs = [f32(14, 4, 8, 512), f32(10, 4, 8, 512), f32(8, parts, 2, 2, 4, 256), f32(256, 128)]
        state = [f32(14, 4, 8, 512)] * 2
        scratch = [(14, 4, 8, 512)] * 3
        body = functools.partial(fine_down_kernel, first)
        if first:
            rhs0, field0, low, edge, cond0, inv0 = call(body, outs + state, scratch, *args, name="fine_down_first")
        else:
            cond0, inv0 = kept[0:2]
            rhs0, field0, low, edge = call(body, outs, scratch, *args, inv0, name="fine_down")
        rows = lax.all_to_all(low, "gy", split_axis=0, concat_axis=0, tiled=True)
        (rows,) = call(pick_kernel, [f32(5, parts, 2, 2, 4, 256)], [], prm, rows, name="pick")
        chip = cores(rows)
        far = cores(pick(across(chip), core))
        near_rows = 192 + (64 if first else 0) + 48 * parts
        outs = [f32(12, 2, 24, 256), f32(8, 2, 24, 256), f32(parts, 2, 24, 128), f32(near_rows, 128)]
        state = [f32(12, 2, 24, 256)] * 2
        scratch = [(12, 2, 24, 256)] * 3
        body = functools.partial(middle_down_kernel, first)
        if first:
            rhs1, field1, low, near, cond1, inv1 = call(
                body, outs + state, scratch, prm, chip, far, name="middle_down_first"
            )
        else:
            cond1, inv1 = kept[2:4]
            rhs1, field1, low, near = call(body, outs, scratch, prm, chip, far, inv1, name="middle_down")
        flat = low.reshape(48 * parts, 128)
        beside = [swap(near, 1), swap(flat, 3), swap(flat, 5)]
        far = cores(jnp.concatenate([edge, *beside], axis=0))
        outs = [f32(4, 4, 4, 512)] * 2
        scratch = [(14, 1, 24, 128)] * 4 + [(14, 2, 16, 256)] + [(12, 2, 16, 256)] * 3 + [(12, 4, 8, 512)] * 3
        args = [prm, low, far, field1, rhs1, cond1, inv1, field0, rhs0, cond0, inv0]
        body = functools.partial(up_kernel, first)
        if first:
            state = [f32(14, 2, 16, 256), f32(14, 1, 24, 128), f32(14, 1, 24, 128)]
            adjoint, remain, *coarse = call(body, outs + state, scratch, *args, name="up_first")
            kept = (cond0, inv0, cond1, inv1, *coarse)
        else:
            adjoint, remain = call(body, outs, scratch, *args, *kept[4:7], adjoint, name="up")
    return tuple(
        call(
            finish_kernel,
            [f32(4, 16, 512)] * 2,
            [(4, 128, 128)],
            adjoint,
            remain,
            scalars=False,
            name="finish",
        )
    )


def solution(mesh):
    placed = (P("gz", "gy", None), P("gz", "gy", None))
    return jax.shard_map(local, mesh=mesh, in_specs=placed, out_specs=placed, check_vma=False)
```

```python
import functools

import jax
import jax.numpy as jnp
from jax import lax
from jax.experimental import pallas as pl
from jax.experimental.pallas import tpu as pltpu
from jax.sharding import PartitionSpec as P

DEGREE = 3
COARSE_DEGREE = 4
CYCLES = 2

CHEB_LOW = 0.3
CHEB_HIGH = 1.9
SCALES = (4.0, 1.0, 0.25)
LANES = 128
VMEM_LIMIT = 16 * 1024 * 1024


def chebyshev(steps):
    theta = (CHEB_HIGH + CHEB_LOW) / 2.0
    delta = (CHEB_HIGH - CHEB_LOW) / 2.0
    sigma = theta / delta
    rho = 1.0 / sigma
    pairs = [(0.0, 1.0 / theta)]
    for _ in range(steps - 1):
        rho_next = 1.0 / (2.0 * sigma - rho)
        pairs.append((rho_next * rho, 2.0 * rho_next / delta))
        rho = rho_next
    return pairs


def lanes(c):
    return slice(c * LANES, (c + 1) * LANES)


def load(ref, z, size):
    return [[ref[z, d, :, lanes(c)] for c in range(size)] for d in range(size)]


def load_ends(ref, z, size):
    top = ref.shape[2]
    return [
        [
            jnp.concatenate([ref[z, d, 0:8, lanes(c)], ref[z, d, top - 8 : top, lanes(c)]], axis=0)
            for c in range(size)
        ]
        for d in range(size)
    ]


def pack(ref, row, tiles):
    for d in range(2):
        for c in range(2):
            at = row + 16 * (2 * d + c)
            ref[at : at + 16, :] = tiles[d][c]


def unpack(ref, core, row):
    return [[ref[core, row + 16 * (2 * d + c) : row + 16 * (2 * d + c) + 16, :] for c in range(2)] for d in range(2)]


def store(ref, z, tiles):
    for d, line in enumerate(tiles):
        for c, tile in enumerate(line):
            ref[z, d, :, lanes(c)] = tile


def neighbours(below, here, above, size):
    rows = here[0][0].shape[0]
    lane = lax.broadcasted_iota(jnp.int32, (rows, LANES), 1)
    first, last = lane == 0, lane == LANES - 1
    out = []
    for d in range(size):
        line = []
        for c in range(size):
            if c > 0:
                left = here[d][c - 1]
            else:
                left = jnp.where(first, 0.0, pltpu.roll(here[d][size - 1], 1, 1))
            if c < size - 1:
                right = here[d][c + 1]
            else:
                right = jnp.where(last, 0.0, pltpu.roll(here[d][0], LANES - 1, 1))
            low = here[d - 1][c] if d > 0 else pltpu.roll(here[size - 1][c], 1, 0)
            high = here[d + 1][c] if d < size - 1 else pltpu.roll(here[0][c], rows - 1, 0)
            line.append(((below[d][c] + above[d][c]) + (left + right)) + (low + high))
        out.append(line)
    return out


def first_step(lo, hi, rhs, inv, w, dw, size, beta):
    for z in range(lo, hi):
        for d in range(size):
            for c in range(size):
                value = (beta * rhs[z, d, :, lanes(c)]) * inv[z, d, :, lanes(c)]
                w[z, d, :, lanes(c)] = value
                dw[z, d, :, lanes(c)] = value


def sweep(lo, hi, src, dst, dst_shift, dw, rhs, inv, shift, size, scale, alpha, beta, loader=load):
    planes = {z: load(src, z, size) for z in range(lo - 1, hi + 1)}
    for z in range(lo, hi):
        here = planes[z]
        near = neighbours(planes[z - 1], here, planes[z + 1], size)
        f = loader(rhs, z + shift, size)
        i = loader(inv, z + shift, size)
        for d in range(size):
            for c in range(size):
                q = i[d][c] * (f[d][c] + scale * near[d][c]) - here[d][c]
                change = beta * q
                if alpha != 0.0:
                    change = change + alpha * dw[z, d, :, lanes(c)]
                dw[z, d, :, lanes(c)] = change
                dst[z + dst_shift, d, :, lanes(c)] = here[d][c] + change


def residual_plane(src, z, rhs, inv, zr, size, scale):
    here = load(src, z, size)
    near = neighbours(load(src, z - 1, size), here, load(src, z + 1, size), size)
    out = []
    for d in range(size):
        line = []
        for c in range(size):
            i = inv[zr, d, :, lanes(c)]
            line.append((rhs[zr, d, :, lanes(c)] + scale * near[d][c]) - here[d][c] / i)
        out.append(line)
    return out


def halve(one, two, size):
    half = size // 2
    return [
        [
            0.125
            * (
                ((one[2 * d][2 * c] + one[2 * d][2 * c + 1]) + (one[2 * d + 1][2 * c] + one[2 * d + 1][2 * c + 1]))
                + ((two[2 * d][2 * c] + two[2 * d][2 * c + 1]) + (two[2 * d + 1][2 * c] + two[2 * d + 1][2 * c + 1]))
            )
            for c in range(half)
        ]
        for d in range(half)
    ]


def inverse_of(cond, scale):
    return 1.0 / (1.0 / cond + 6.0 * scale)


def selector(to_tiles):
    rows = lax.broadcasted_iota(jnp.int32, (512, 512), 0)
    cols = lax.broadcasted_iota(jnp.int32, (512, 512), 1)
    if to_tiles:
        hit = rows == 4 * (cols % LANES) + cols // LANES
    else:
        hit = cols == 4 * (rows % LANES) + rows // LANES
    return jnp.where(hit, 1.0, 0.0).astype(jnp.float32)


def reorder(rows, to_tiles):
    return jnp.dot(
        rows, selector(to_tiles), precision=lax.Precision.HIGHEST, preferred_element_type=jnp.float32
    )


def prepare_kernel(source, cond, out, both, work, sems):
    copies = [pltpu.make_async_copy(ref, both.at[a], sems.at[a]) for a, ref in enumerate((source, cond))]
    for copy in copies:
        copy.start()
    for copy in copies:
        copy.wait()
    tiles = reorder(both[...].reshape(128, 512), True)
    for c in range(4):
        work[c] = tiles[:, lanes(c)]
    for a in range(2):
        for z in range(4):
            for d in range(4):
                for c in range(4):
                    out[z, 4 * a + d, :, lanes(c)] = work[c, pl.ds(64 * a + 16 * z + d, 4, stride=4), :]


def finish_kernel(adjoint, remain, out_a, out_r, work):
    for a, ref in enumerate((adjoint, remain)):
        for z in range(4):
            for d in range(4):
                for c in range(4):
                    work[c, pl.ds(64 * a + 16 * z + d, 4, stride=4), :] = ref[z, d, :, lanes(c)]
    rows = reorder(jnp.concatenate([work[c] for c in range(4)], axis=1), False)
    out_a[...] = rows[0:64].reshape(4, 16, 512)
    out_r[...] = rows[64:128].reshape(4, 16, 512)


def rows_kernel(parts, prm, chip, halves, *outs):
    core, odd = prm[0], prm[1]
    for a in range(parts):
        whole, send = outs[2 * a : 2 * a + 2]
        for t in range(8):
            for d in range(4):
                whole[t, d, 0:4, :] = chip[t // 4, t % 4, 4 * a + d]
                whole[t, d, 4:6, :] = halves[odd, t, 4 * a + d]
                whole[t, d, 6:8, :] = halves[1 - odd, t, 4 * a + d]
        for t in range(6):
            send[t] = whole[2 * core + t]


def fine_down_kernel(first, prm, *refs):
    if first:
        whole, side, whole_k, side_k, rhs, field, low, edge, cond, inv, wa, wb, dw = refs
    else:
        whole, side, inv, rhs, field, low, edge, wa, wb, dw = refs
    core = prm[0]

    @pl.when(core == 0)
    def _():
        for t in range(6):
            rhs[t] = side[0, t]
            if first:
                cond[t] = side_k[t]
        for t in range(8):
            rhs[6 + t] = whole[t]
            if first:
                cond[6 + t] = whole_k[t]

    @pl.when(core == 1)
    def _():
        for t in range(8):
            rhs[t] = whole[t]
            if first:
                cond[t] = whole_k[t]
        for t in range(6):
            rhs[8 + t] = side[1, t]
            if first:
                cond[8 + t] = side_k[t]

    if first:
        for t in range(14):
            inv[t] = inverse_of(cond[t], SCALES[0])
    steps = chebyshev(DEGREE)
    first_step(0, 14, rhs, inv, wa, dw, 4, steps[0][1])
    sweep(1, 13, wa, wb, 0, dw, rhs, inv, 0, 4, SCALES[0], *steps[1])
    sweep(2, 12, wb, field, -2, dw, rhs, inv, 0, 4, SCALES[0], *steps[2])
    for q in range(2):
        for d in range(4):
            for c in range(4):
                row = 8 * ((q * 4 + d) * 4 + c)
                edge[row : row + 8, :] = field[4 + q, d, :, lanes(c)]
    for t in range(2):
        z = 6 - 2 * core + 2 * t
        one = residual_plane(field, z - 2, rhs, inv, z, 4, SCALES[0])
        two = residual_plane(field, z - 1, rhs, inv, z + 1, 4, SCALES[0])
        mean = halve(one, two, 4)
        for d in range(2):
            for c in range(2):
                for r in range(8):
                    low[r, 0, t, d, :, lanes(c)] = mean[d][c][0:4]
        if first:
            mean = halve(load(cond, z, 4), load(cond, z + 1, 4), 4)
            for d in range(2):
                for c in range(2):
                    for r in range(8):
                        low[r, 1, t, d, :, lanes(c)] = mean[d][c][0:4]


def pick_kernel(prm, rows, out):
    for j, step in enumerate((0, 1, 2, 6, 7)):
        out[j] = rows[lax.rem(prm[2] + step, 8)]


def middle_down_kernel(first, prm, chip, far, *refs):
    if first:
        rhs, field, low, near, cond, inv, wa, wb, dw = refs
    else:
        inv, rhs, field, low, near, wa, wb, dw = refs
    core = prm[0]
    for t in range(12):
        if t < 4:
            ref, at = far.at[0], t
        elif t < 8:
            ref, at = chip, t - 4
        else:
            ref, at = far.at[1], t - 8
        for d in range(2):
            for j, row in enumerate((0, 4, 8, 16, 20)):
                rhs[t, d, row : row + 4, :] = ref[at // 2, j, 0, at % 2, d]
                if first:
                    cond[t, d, row : row + 4, :] = ref[at // 2, j, 1, at % 2, d]
            rhs[t, d, 12:16, :] = jnp.zeros((4, 256), jnp.float32)
            if first:
                cond[t, d, 12:16, :] = jnp.ones((4, 256), jnp.float32)
    if first:
        for t in range(12):
            inv[t] = inverse_of(cond[t], SCALES[1])
    steps = chebyshev(DEGREE)
    first_step(0, 12, rhs, inv, wa, dw, 2, steps[0][1])
    sweep(1, 11, wa, wb, 0, dw, rhs, inv, 0, 2, SCALES[1], *steps[1])
    sweep(2, 10, wb, field, -2, dw, rhs, inv, 0, 2, SCALES[1], *steps[2])
    for h in range(2):
        z = 4 + 2 * h
        one = residual_plane(field, z - 2, rhs, inv, z, 2, SCALES[1])
        two = residual_plane(field, z - 1, rhs, inv, z + 1, 2, SCALES[1])
        low[0, h] = halve(one, two, 2)[0][0]
        if first:
            low[1, h] = halve(load(cond, z, 2), load(cond, z + 1, 2), 2)[0][0]
    for t in range(3):
        pack(near, 64 * t, load_ends(field, 4 - 3 * core + t, 2))
    at = 192
    if first:
        pack(near, at, load_ends(cond, 8 - 5 * core, 2))
        at += 64
    for a in range(2 if first else 1):
        for h in range(2):
            row = at + 48 * a + 24 * h
            near[row : row + 24, :] = low[a, h]


def up_kernel(first, prm, low, far, middle, mid_rhs, mid_cond, mid_inv, fine, rhs, cond, inv, *refs):
    if first:
        adjoint, remain, ends, low_cond, low_inv = refs[:5]
    else:
        ends, low_cond, low_inv, before, adjoint, remain = refs[:6]
    low_rhs, la, lb, ldw, start, mid_a, mid_b, mid_dw, wa, wb, dw = refs[-11:]
    core = prm[0]
    parts = 2 if first else 1
    base = 256 + 192 + (64 if first else 0)

    for a in range(parts):
        for t in range(14):
            if t < 6:
                row = base + 48 * parts * (2 - t // 2) + 48 * a + 24 * (t % 2)
                value = far[0, row : row + 24, :]
            elif t < 8:
                value = low[a, t - 6]
            else:
                row = base + 48 * parts * (t // 2 - 4) + 48 * a + 24 * (t % 2)
                value = far[1, row : row + 24, :]
            if a == 0:
                low_rhs[t, 0] = value
            else:
                low_cond[t, 0] = value
                low_inv[t, 0] = inverse_of(value, SCALES[2])
    steps = chebyshev(COARSE_DEGREE)
    first_step(0, 14, low_rhs, low_inv, la, ldw, 1, steps[0][1])
    sweep(1, 13, la, lb, 0, ldw, low_rhs, low_inv, 0, 1, SCALES[2], *steps[1])
    sweep(2, 12, lb, la, 0, ldw, low_rhs, low_inv, 0, 1, SCALES[2], *steps[2])
    sweep(3, 11, la, lb, 0, ldw, low_rhs, low_inv, 0, 1, SCALES[2], *steps[3])

    for t in range(3):
        store(start, t, unpack(far, 0, 256 + 64 * t))
        store(start, 11 + t, unpack(far, 1, 256 + 64 * t))
    for t in range(8):
        store(start, 3 + t, load_ends(middle, t, 2))
    if first:
        store(ends, 0, unpack(far, 0, 448))
        store(ends, 13, unpack(far, 1, 448))
        for t in range(12):
            store(ends, 1 + t, load_ends(mid_cond, t, 2))
    for t in range(12):
        at = (t + 1) // 2 + 3 + core
        value = lb[at, 0] / low_cond[at, 0]
        value = jnp.concatenate([value[0:8], value[16:24]], axis=0)
        here = load(start, t + 2 * core, 2)
        k = load(ends, t + 2 * core, 2)
        store(mid_a, t, [[here[d][c] + k[d][c] * value for c in range(2)] for d in range(2)])

    def beyond(other, at):
        for q in range(2):
            for d in range(4):
                for c in range(4):
                    row = 8 * ((q * 4 + d) * 4 + c)
                    wa[at + q, d, :, lanes(c)] = far[other, row : row + 8, :]

    @pl.when(core == 0)
    def _():
        for t in range(10):
            wa[t] = fine[t]
        beyond(1, 10)

    @pl.when(core == 1)
    def _():
        for t in range(10):
            wa[2 + t] = fine[t]
        beyond(0, 0)

    steps = chebyshev(DEGREE)
    shift = 2 * core - 1
    sweep(1, 11, mid_a, mid_b, 0, mid_dw, mid_rhs, mid_inv, shift, 2, SCALES[1], *steps[0], loader=load_ends)
    sweep(2, 10, mid_b, mid_a, 0, mid_dw, mid_rhs, mid_inv, shift, 2, SCALES[1], *steps[1], loader=load_ends)
    sweep(3, 9, mid_a, mid_b, 0, mid_dw, mid_rhs, mid_inv, shift, 2, SCALES[1], *steps[2], loader=load_ends)

    near = lax.broadcasted_iota(jnp.int32, (8, LANES), 0) < 6
    ahead = 2 - 2 * core

    for t in range(3, 9):
        k = load(ends, t + 2 * core, 2)
        for d in range(2):
            for c in range(2):
                value = mid_b[t, d, :, lanes(c)] / k[d][c]
                value = jnp.where(near, value[0:8], value[8:16])
                for z in range(2):
                    v = 2 * (t - 3) + z
                    for dd in (2 * d, 2 * d + 1):
                        for cc in (2 * c, 2 * c + 1):
                            wa[v, dd, :, lanes(cc)] = (
                                wa[v, dd, :, lanes(cc)] + cond[v + ahead, dd, :, lanes(cc)] * value
                            )

    sweep(1, 11, wa, wb, 0, dw, rhs, inv, ahead, 4, SCALES[0], *steps[0])
    sweep(2, 10, wb, wa, 0, dw, rhs, inv, ahead, 4, SCALES[0], *steps[1])
    sweep(3, 9, wa, wb, 0, dw, rhs, inv, ahead, 4, SCALES[0], *steps[2])

    for t in range(4):
        left = residual_plane(wb, t + 4, rhs, inv, t + 4 + ahead, 4, SCALES[0])
        for d in range(4):
            for c in range(4):
                value = wb[t + 4, d, :, lanes(c)] / cond[t + 4 + ahead, d, :, lanes(c)]
                value = value[0:4]
                if not first:
                    value = value + before[t, d, :, lanes(c)]
                adjoint[t, d, :, lanes(c)] = value
                remain[t, d, :, lanes(c)] = left[d][c][0:4]


def f32(*shape):
    return jax.ShapeDtypeStruct(shape, jnp.float32)


def call(body, outs, scratch, *args, scalars=True, space=pltpu.VMEM, sems=0, limit=VMEM_LIMIT, name=None):
    specs = [pl.BlockSpec(memory_space=space)] * len(args)
    if scalars:
        specs[0] = pl.BlockSpec(memory_space=pltpu.SMEM)
    return pl.pallas_call(
        body,
        out_shape=outs,
        in_specs=specs,
        out_specs=[pl.BlockSpec(memory_space=pltpu.VMEM)] * len(outs),
        scratch_shapes=[pltpu.VMEM(s, jnp.float32) for s in scratch]
        + ([pltpu.SemaphoreType.DMA((sems,))] if sems else []),
        compiler_params=pltpu.CompilerParams(vmem_limit_bytes=limit),
        name=name,
    )(*args)


def pairs(first, step, size):
    devices = lax.axis_size("gz")
    return [[(b + i) % devices, (b + i + step) % devices] for b in range(0, devices, size) for i in first]


def gather(value, first, step, size):
    return lax.all_gather(value, "gz", axis_index_groups=pairs(first, step, size))


def cores(value):
    return gather(value, (0,), 1, 2)


def across(value):
    return gather(value, (1,), 1, 2)


def swap(value, step):
    devices = lax.axis_size("gz")
    ways = []
    for i in range(1, devices, 2):
        ways += [(i, (i + step) % devices), ((i + step) % devices, i)]
    return lax.ppermute(value, "gz", ways)


def row_pairs(value):
    planes, rows = lax.axis_size("gz"), lax.axis_size("gy")
    members = []
    for z in range(planes):
        for y in range(z % 2, rows, 2):
            members.append([z * rows + y, z * rows + (y + 1) % rows])
    return lax.all_gather(value, ("gz", "gy"), axis_index_groups=members)


def pick(value, index):
    return lax.dynamic_index_in_dim(value, index, 0, keepdims=False)


def local(source, conduct):
    z = lax.axis_index("gz").astype(jnp.uint32)
    y = lax.axis_index("gy").astype(jnp.uint32)
    core = z % 2
    prm = jnp.stack([core, y % 2, y, z]).astype(jnp.int32)
    place = (core + y) % 2
    (remain,) = call(
        prepare_kernel,
        [f32(4, 8, 4, 512)],
        [(2, 4, 16, 512), (4, 128, 128)],
        source,
        conduct,
        scalars=False,
        space=pl.ANY,
        sems=2,
        limit=60 * 1024 * 1024,
        name="prepare",
    )
    adjoint = None
    kept = None
    for cycle in range(CYCLES):
        first = cycle == 0
        parts = 2 if first else 1
        chip = cores(remain)
        flat = chip.reshape(8, *chip.shape[2:])
        halves = row_pairs(jnp.where(place == 0, flat[:, :, 2:4], flat[:, :, 0:2]))
        halves = cores(jnp.where(place == 0, halves[1], halves[0]))
        laid = call(
            functools.partial(rows_kernel, parts),
            [f32(8, 4, 8, 512), f32(6, 4, 8, 512)] * parts,
            [],
            prm,
            chip,
            halves,
            name="rows",
        )
        args = [prm]
        if first:
            side_k = swap(laid[3], 1)
        args += [laid[0], across(laid[1])]
        if first:
            args += [laid[2], side_k]
        outs = [f32(14, 4, 8, 512), f32(10, 4, 8, 512), f32(8, parts, 2, 2, 4, 256), f32(256, 128)]
        state = [f32(14, 4, 8, 512)] * 2
        scratch = [(14, 4, 8, 512)] * 3
        body = functools.partial(fine_down_kernel, first)
        if first:
            rhs0, field0, low, edge, cond0, inv0 = call(body, outs + state, scratch, *args, name="fine_down_first")
        else:
            cond0, inv0 = kept[0:2]
            rhs0, field0, low, edge = call(body, outs, scratch, *args, inv0, name="fine_down")
        rows = lax.all_to_all(low, "gy", split_axis=0, concat_axis=0, tiled=True)
        (rows,) = call(pick_kernel, [f32(5, parts, 2, 2, 4, 256)], [], prm, rows, name="pick")
        chip = cores(rows)
        far = cores(pick(across(chip), core))
        near_rows = 192 + (64 if first else 0) + 48 * parts
        outs = [f32(12, 2, 24, 256), f32(8, 2, 24, 256), f32(parts, 2, 24, 128), f32(near_rows, 128)]
        state = [f32(12, 2, 24, 256)] * 2
        scratch = [(12, 2, 24, 256)] * 3
        body = functools.partial(middle_down_kernel, first)
        if first:
            rhs1, field1, low, near, cond1, inv1 = call(
                body, outs + state, scratch, prm, chip, far, name="middle_down_first"
            )
        else:
            cond1, inv1 = kept[2:4]
            rhs1, field1, low, near = call(body, outs, scratch, prm, chip, far, inv1, name="middle_down")
        flat = low.reshape(48 * parts, 128)
        beside = [swap(near, 1), swap(flat, 3), swap(flat, 5)]
        far = cores(jnp.concatenate([edge, *beside], axis=0))
        outs = [f32(4, 4, 4, 512)] * 2
        scratch = [(14, 1, 24, 128)] * 4 + [(14, 2, 16, 256)] + [(12, 2, 16, 256)] * 3 + [(12, 4, 8, 512)] * 3
        args = [prm, low, far, field1, rhs1, cond1, inv1, field0, rhs0, cond0, inv0]
        body = functools.partial(up_kernel, first)
        if first:
            state = [f32(14, 2, 16, 256), f32(14, 1, 24, 128), f32(14, 1, 24, 128)]
            adjoint, remain, *coarse = call(body, outs + state, scratch, *args, name="up_first")
            kept = (cond0, inv0, cond1, inv1, *coarse)
        else:
            adjoint, remain = call(body, outs, scratch, *args, *kept[4:7], adjoint, name="up")
    return tuple(
        call(
            finish_kernel,
            [f32(4, 16, 512)] * 2,
            [(4, 128, 128)],
            adjoint,
            remain,
            scalars=False,
            name="finish",
        )
    )


def solution(mesh):
    placed = (P("gz", "gy", None), P("gz", "gy", None))
    return jax.shard_map(local, mesh=mesh, in_specs=placed, out_specs=placed, check_vma=False)
```

```python
import functools

import jax
import jax.numpy as jnp
from jax import lax
from jax.experimental import pallas as pl
from jax.experimental.pallas import tpu as pltpu
from jax.sharding import PartitionSpec as P

DEGREE = 3
COARSE_DEGREE = 4
CYCLES = 2

CHEB_LOW = 0.3
CHEB_HIGH = 1.9
SCALES = (4.0, 1.0, 0.25)
LANES = 128
VMEM_LIMIT = 16 * 1024 * 1024


def chebyshev(steps):
    theta = (CHEB_HIGH + CHEB_LOW) / 2.0
    delta = (CHEB_HIGH - CHEB_LOW) / 2.0
    sigma = theta / delta
    rho = 1.0 / sigma
    pairs = [(0.0, 1.0 / theta)]
    for _ in range(steps - 1):
        rho_next = 1.0 / (2.0 * sigma - rho)
        pairs.append((rho_next * rho, 2.0 * rho_next / delta))
        rho = rho_next
    return pairs


def lanes(c):
    return slice(c * LANES, (c + 1) * LANES)


def load(ref, z, size):
    return [[ref[z, d, :, lanes(c)] for c in range(size)] for d in range(size)]


def load_ends(ref, z, size):
    top = ref.shape[2]
    return [
        [
            jnp.concatenate([ref[z, d, 0:8, lanes(c)], ref[z, d, top - 8 : top, lanes(c)]], axis=0)
            for c in range(size)
        ]
        for d in range(size)
    ]


def pack(ref, row, tiles):
    for d in range(2):
        for c in range(2):
            at = row + 16 * (2 * d + c)
            ref[at : at + 16, :] = tiles[d][c]


def unpack(ref, core, row):
    return [[ref[core, row + 16 * (2 * d + c) : row + 16 * (2 * d + c) + 16, :] for c in range(2)] for d in range(2)]


def store(ref, z, tiles):
    for d, line in enumerate(tiles):
        for c, tile in enumerate(line):
            ref[z, d, :, lanes(c)] = tile


def neighbours(below, here, above, size):
    rows = here[0][0].shape[0]
    lane = lax.broadcasted_iota(jnp.int32, (rows, LANES), 1)
    first, last = lane == 0, lane == LANES - 1
    out = []
    for d in range(size):
        line = []
        for c in range(size):
            if c > 0:
                left = here[d][c - 1]
            else:
                left = jnp.where(first, 0.0, pltpu.roll(here[d][size - 1], 1, 1))
            if c < size - 1:
                right = here[d][c + 1]
            else:
                right = jnp.where(last, 0.0, pltpu.roll(here[d][0], LANES - 1, 1))
            low = here[d - 1][c] if d > 0 else pltpu.roll(here[size - 1][c], 1, 0)
            high = here[d + 1][c] if d < size - 1 else pltpu.roll(here[0][c], rows - 1, 0)
            line.append(((below[d][c] + above[d][c]) + (left + right)) + (low + high))
        out.append(line)
    return out


def first_step(lo, hi, rhs, inv, w, dw, size, beta):
    for z in range(lo, hi):
        for d in range(size):
            for c in range(size):
                value = (beta * rhs[z, d, :, lanes(c)]) * inv[z, d, :, lanes(c)]
                w[z, d, :, lanes(c)] = value
                dw[z, d, :, lanes(c)] = value


def sweep(lo, hi, src, dst, dst_shift, dw, rhs, inv, shift, size, scale, alpha, beta, loader=load):
    planes = {z: load(src, z, size) for z in range(lo - 1, hi + 1)}
    for z in range(lo, hi):
        here = planes[z]
        near = neighbours(planes[z - 1], here, planes[z + 1], size)
        f = loader(rhs, z + shift, size)
        i = loader(inv, z + shift, size)
        for d in range(size):
            for c in range(size):
                q = i[d][c] * (f[d][c] + scale * near[d][c]) - here[d][c]
                change = beta * q
                if alpha != 0.0:
                    change = change + alpha * dw[z, d, :, lanes(c)]
                dw[z, d, :, lanes(c)] = change
                dst[z + dst_shift, d, :, lanes(c)] = here[d][c] + change


def residual_plane(src, z, rhs, inv, zr, size, scale):
    here = load(src, z, size)
    near = neighbours(load(src, z - 1, size), here, load(src, z + 1, size), size)
    out = []
    for d in range(size):
        line = []
        for c in range(size):
            i = inv[zr, d, :, lanes(c)]
            line.append((rhs[zr, d, :, lanes(c)] + scale * near[d][c]) - here[d][c] / i)
        out.append(line)
    return out


def halve(one, two, size):
    half = size // 2
    return [
        [
            0.125
            * (
                ((one[2 * d][2 * c] + one[2 * d][2 * c + 1]) + (one[2 * d + 1][2 * c] + one[2 * d + 1][2 * c + 1]))
                + ((two[2 * d][2 * c] + two[2 * d][2 * c + 1]) + (two[2 * d + 1][2 * c] + two[2 * d + 1][2 * c + 1]))
            )
            for c in range(half)
        ]
        for d in range(half)
    ]


def inverse_of(cond, scale):
    return 1.0 / (1.0 / cond + 6.0 * scale)


def selector(to_tiles):
    rows = lax.broadcasted_iota(jnp.int32, (512, 512), 0)
    cols = lax.broadcasted_iota(jnp.int32, (512, 512), 1)
    if to_tiles:
        hit = rows == 4 * (cols % LANES) + cols // LANES
    else:
        hit = cols == 4 * (rows % LANES) + rows // LANES
    return jnp.where(hit, 1.0, 0.0).astype(jnp.float32)


def reorder(rows, to_tiles):
    return jnp.dot(
        rows, selector(to_tiles), precision=lax.Precision.HIGHEST, preferred_element_type=jnp.float32
    )


def prepare_kernel(source, cond, out, work):
    rows = jnp.concatenate([source[...].reshape(64, 512), cond[...].reshape(64, 512)], axis=0)
    tiles = reorder(rows, True)
    for c in range(4):
        work[c] = tiles[:, lanes(c)]
    for a in range(2):
        for z in range(4):
            for d in range(4):
                for c in range(4):
                    out[z, 4 * a + d, :, lanes(c)] = work[c, pl.ds(64 * a + 16 * z + d, 4, stride=4), :]


def finish_kernel(adjoint, remain, out_a, out_r, work):
    for a, ref in enumerate((adjoint, remain)):
        for z in range(4):
            for d in range(4):
                for c in range(4):
                    work[c, pl.ds(64 * a + 16 * z + d, 4, stride=4), :] = ref[z, d, :, lanes(c)]
    rows = reorder(jnp.concatenate([work[c] for c in range(4)], axis=1), False)
    out_a[...] = rows[0:64].reshape(4, 16, 512)
    out_r[...] = rows[64:128].reshape(4, 16, 512)


def rows_kernel(parts, prm, chip, halves, *outs):
    core, odd = prm[0], prm[1]
    for a in range(parts):
        whole, send = outs[2 * a : 2 * a + 2]
        for t in range(8):
            for d in range(4):
                whole[t, d, 0:4, :] = chip[t // 4, t % 4, 4 * a + d]
                whole[t, d, 4:6, :] = halves[odd, t, 4 * a + d]
                whole[t, d, 6:8, :] = halves[1 - odd, t, 4 * a + d]
        for t in range(6):
            send[t] = whole[2 * core + t]


def fine_down_kernel(first, prm, *refs):
    if first:
        whole, side, whole_k, side_k, rhs, field, low, edge, cond, inv, wa, wb, dw = refs
    else:
        whole, side, inv, rhs, field, low, edge, wa, wb, dw = refs
    core = prm[0]

    @pl.when(core == 0)
    def _():
        for t in range(6):
            rhs[t] = side[0, t]
            if first:
                cond[t] = side_k[t]
        for t in range(8):
            rhs[6 + t] = whole[t]
            if first:
                cond[6 + t] = whole_k[t]

    @pl.when(core == 1)
    def _():
        for t in range(8):
            rhs[t] = whole[t]
            if first:
                cond[t] = whole_k[t]
        for t in range(6):
            rhs[8 + t] = side[1, t]
            if first:
                cond[8 + t] = side_k[t]

    if first:
        for t in range(14):
            inv[t] = inverse_of(cond[t], SCALES[0])
    steps = chebyshev(DEGREE)
    first_step(0, 14, rhs, inv, wa, dw, 4, steps[0][1])
    sweep(1, 13, wa, wb, 0, dw, rhs, inv, 0, 4, SCALES[0], *steps[1])
    sweep(2, 12, wb, field, -2, dw, rhs, inv, 0, 4, SCALES[0], *steps[2])
    for q in range(2):
        for d in range(4):
            for c in range(4):
                row = 8 * ((q * 4 + d) * 4 + c)
                edge[row : row + 8, :] = field[4 + q, d, :, lanes(c)]
    for t in range(2):
        z = 6 - 2 * core + 2 * t
        one = residual_plane(field, z - 2, rhs, inv, z, 4, SCALES[0])
        two = residual_plane(field, z - 1, rhs, inv, z + 1, 4, SCALES[0])
        mean = halve(one, two, 4)
        for d in range(2):
            for c in range(2):
                for r in range(8):
                    low[r, 0, t, d, :, lanes(c)] = mean[d][c][0:4]
        if first:
            mean = halve(load(cond, z, 4), load(cond, z + 1, 4), 4)
            for d in range(2):
                for c in range(2):
                    for r in range(8):
                        low[r, 1, t, d, :, lanes(c)] = mean[d][c][0:4]


def pick_kernel(prm, rows, out):
    for j, step in enumerate((0, 1, 2, 6, 7)):
        out[j] = rows[lax.rem(prm[2] + step, 8)]


def middle_down_kernel(first, prm, chip, far, *refs):
    if first:
        rhs, field, low, near, cond, inv, wa, wb, dw = refs
    else:
        inv, rhs, field, low, near, wa, wb, dw = refs
    core = prm[0]
    for t in range(12):
        if t < 4:
            ref, at = far.at[0], t
        elif t < 8:
            ref, at = chip, t - 4
        else:
            ref, at = far.at[1], t - 8
        for d in range(2):
            for j, row in enumerate((0, 4, 8, 16, 20)):
                rhs[t, d, row : row + 4, :] = ref[at // 2, j, 0, at % 2, d]
                if first:
                    cond[t, d, row : row + 4, :] = ref[at // 2, j, 1, at % 2, d]
            rhs[t, d, 12:16, :] = jnp.zeros((4, 256), jnp.float32)
            if first:
                cond[t, d, 12:16, :] = jnp.ones((4, 256), jnp.float32)
    if first:
        for t in range(12):
            inv[t] = inverse_of(cond[t], SCALES[1])
    steps = chebyshev(DEGREE)
    first_step(0, 12, rhs, inv, wa, dw, 2, steps[0][1])
    sweep(1, 11, wa, wb, 0, dw, rhs, inv, 0, 2, SCALES[1], *steps[1])
    sweep(2, 10, wb, field, -2, dw, rhs, inv, 0, 2, SCALES[1], *steps[2])
    for h in range(2):
        z = 4 + 2 * h
        one = residual_plane(field, z - 2, rhs, inv, z, 2, SCALES[1])
        two = residual_plane(field, z - 1, rhs, inv, z + 1, 2, SCALES[1])
        low[0, h] = halve(one, two, 2)[0][0]
        if first:
            low[1, h] = halve(load(cond, z, 2), load(cond, z + 1, 2), 2)[0][0]
    for t in range(3):
        pack(near, 64 * t, load_ends(field, 4 - 3 * core + t, 2))
    at = 192
    if first:
        pack(near, at, load_ends(cond, 8 - 5 * core, 2))
        at += 64
    for a in range(2 if first else 1):
        for h in range(2):
            row = at + 48 * a + 24 * h
            near[row : row + 24, :] = low[a, h]


def up_kernel(first, prm, low, far, middle, mid_rhs, mid_cond, mid_inv, fine, rhs, cond, inv, *refs):
    if first:
        adjoint, remain, ends, low_cond, low_inv = refs[:5]
    else:
        ends, low_cond, low_inv, before, adjoint, remain = refs[:6]
    low_rhs, la, lb, ldw, start, mid_a, mid_b, mid_dw, wa, wb, dw = refs[-11:]
    core = prm[0]
    parts = 2 if first else 1
    base = 256 + 192 + (64 if first else 0)

    for a in range(parts):
        for t in range(14):
            if t < 6:
                row = base + 48 * parts * (2 - t // 2) + 48 * a + 24 * (t % 2)
                value = far[0, row : row + 24, :]
            elif t < 8:
                value = low[a, t - 6]
            else:
                row = base + 48 * parts * (t // 2 - 4) + 48 * a + 24 * (t % 2)
                value = far[1, row : row + 24, :]
            if a == 0:
                low_rhs[t, 0] = value
            else:
                low_cond[t, 0] = value
                low_inv[t, 0] = inverse_of(value, SCALES[2])
    steps = chebyshev(COARSE_DEGREE)
    first_step(0, 14, low_rhs, low_inv, la, ldw, 1, steps[0][1])
    sweep(1, 13, la, lb, 0, ldw, low_rhs, low_inv, 0, 1, SCALES[2], *steps[1])
    sweep(2, 12, lb, la, 0, ldw, low_rhs, low_inv, 0, 1, SCALES[2], *steps[2])
    sweep(3, 11, la, lb, 0, ldw, low_rhs, low_inv, 0, 1, SCALES[2], *steps[3])

    for t in range(3):
        store(start, t, unpack(far, 0, 256 + 64 * t))
        store(start, 11 + t, unpack(far, 1, 256 + 64 * t))
    for t in range(8):
        store(start, 3 + t, load_ends(middle, t, 2))
    if first:
        store(ends, 0, unpack(far, 0, 448))
        store(ends, 13, unpack(far, 1, 448))
        for t in range(12):
            store(ends, 1 + t, load_ends(mid_cond, t, 2))
    for t in range(12):
        at = (t + 1) // 2 + 3 + core
        value = lb[at, 0] / low_cond[at, 0]
        value = jnp.concatenate([value[0:8], value[16:24]], axis=0)
        here = load(start, t + 2 * core, 2)
        k = load(ends, t + 2 * core, 2)
        store(mid_a, t, [[here[d][c] + k[d][c] * value for c in range(2)] for d in range(2)])

    def beyond(other, at):
        for q in range(2):
            for d in range(4):
                for c in range(4):
                    row = 8 * ((q * 4 + d) * 4 + c)
                    wa[at + q, d, :, lanes(c)] = far[other, row : row + 8, :]

    @pl.when(core == 0)
    def _():
        for t in range(10):
            wa[t] = fine[t]
        beyond(1, 10)

    @pl.when(core == 1)
    def _():
        for t in range(10):
            wa[2 + t] = fine[t]
        beyond(0, 0)

    steps = chebyshev(DEGREE)
    shift = 2 * core - 1
    sweep(1, 11, mid_a, mid_b, 0, mid_dw, mid_rhs, mid_inv, shift, 2, SCALES[1], *steps[0], loader=load_ends)
    sweep(2, 10, mid_b, mid_a, 0, mid_dw, mid_rhs, mid_inv, shift, 2, SCALES[1], *steps[1], loader=load_ends)
    sweep(3, 9, mid_a, mid_b, 0, mid_dw, mid_rhs, mid_inv, shift, 2, SCALES[1], *steps[2], loader=load_ends)

    near = lax.broadcasted_iota(jnp.int32, (8, LANES), 0) < 6
    ahead = 2 - 2 * core

    for t in range(3, 9):
        k = load(ends, t + 2 * core, 2)
        for d in range(2):
            for c in range(2):
                value = mid_b[t, d, :, lanes(c)] / k[d][c]
                value = jnp.where(near, value[0:8], value[8:16])
                for z in range(2):
                    v = 2 * (t - 3) + z
                    for dd in (2 * d, 2 * d + 1):
                        for cc in (2 * c, 2 * c + 1):
                            wa[v, dd, :, lanes(cc)] = (
                                wa[v, dd, :, lanes(cc)] + cond[v + ahead, dd, :, lanes(cc)] * value
                            )

    sweep(1, 11, wa, wb, 0, dw, rhs, inv, ahead, 4, SCALES[0], *steps[0])
    sweep(2, 10, wb, wa, 0, dw, rhs, inv, ahead, 4, SCALES[0], *steps[1])
    sweep(3, 9, wa, wb, 0, dw, rhs, inv, ahead, 4, SCALES[0], *steps[2])

    for t in range(4):
        left = residual_plane(wb, t + 4, rhs, inv, t + 4 + ahead, 4, SCALES[0])
        for d in range(4):
            for c in range(4):
                value = wb[t + 4, d, :, lanes(c)] / cond[t + 4 + ahead, d, :, lanes(c)]
                value = value[0:4]
                if not first:
                    value = value + before[t, d, :, lanes(c)]
                adjoint[t, d, :, lanes(c)] = value
                remain[t, d, :, lanes(c)] = left[d][c][0:4]


def f32(*shape):
    return jax.ShapeDtypeStruct(shape, jnp.float32)


def call(body, outs, scratch, *args, scalars=True, name=None):
    specs = [pl.BlockSpec(memory_space=pltpu.VMEM)] * len(args)
    if scalars:
        specs[0] = pl.BlockSpec(memory_space=pltpu.SMEM)
    return pl.pallas_call(
        body,
        out_shape=outs,
        in_specs=specs,
        out_specs=[pl.BlockSpec(memory_space=pltpu.VMEM)] * len(outs),
        scratch_shapes=[pltpu.VMEM(s, jnp.float32) for s in scratch],
        compiler_params=pltpu.CompilerParams(vmem_limit_bytes=VMEM_LIMIT),
        name=name,
    )(*args)


def pairs(first, step, size):
    devices = lax.axis_size("gz")
    return [[(b + i) % devices, (b + i + step) % devices] for b in range(0, devices, size) for i in first]


def gather(value, first, step, size):
    return lax.all_gather(value, "gz", axis_index_groups=pairs(first, step, size))


def cores(value):
    return gather(value, (0,), 1, 2)


def across(value):
    return gather(value, (1,), 1, 2)


def swap(value, step):
    devices = lax.axis_size("gz")
    ways = []
    for i in range(1, devices, 2):
        ways += [(i, (i + step) % devices), ((i + step) % devices, i)]
    return lax.ppermute(value, "gz", ways)


def row_pairs(value):
    planes, rows = lax.axis_size("gz"), lax.axis_size("gy")
    members = []
    for z in range(planes):
        for y in range(z % 2, rows, 2):
            members.append([z * rows + y, z * rows + (y + 1) % rows])
    return lax.all_gather(value, ("gz", "gy"), axis_index_groups=members)


def pick(value, index):
    return lax.dynamic_index_in_dim(value, index, 0, keepdims=False)


def local(source, conduct):
    z = lax.axis_index("gz").astype(jnp.uint32)
    y = lax.axis_index("gy").astype(jnp.uint32)
    core = z % 2
    prm = jnp.stack([core, y % 2, y, z]).astype(jnp.int32)
    place = (core + y) % 2
    (remain,) = call(
        prepare_kernel,
        [f32(4, 8, 4, 512)],
        [(4, 128, 128)],
        source,
        conduct,
        scalars=False,
        name="prepare",
    )
    adjoint = None
    kept = None
    for cycle in range(CYCLES):
        first = cycle == 0
        parts = 2 if first else 1
        chip = cores(remain)
        flat = chip.reshape(8, *chip.shape[2:])
        halves = row_pairs(jnp.where(place == 0, flat[:, :, 2:4], flat[:, :, 0:2]))
        halves = cores(jnp.where(place == 0, halves[1], halves[0]))
        laid = call(
            functools.partial(rows_kernel, parts),
            [f32(8, 4, 8, 512), f32(6, 4, 8, 512)] * parts,
            [],
            prm,
            chip,
            halves,
            name="rows",
        )
        args = [prm]
        if first:
            side_k = swap(laid[3], 1)
        args += [laid[0], across(laid[1])]
        if first:
            args += [laid[2], side_k]
        outs = [f32(14, 4, 8, 512), f32(10, 4, 8, 512), f32(8, parts, 2, 2, 4, 256), f32(256, 128)]
        state = [f32(14, 4, 8, 512)] * 2
        scratch = [(14, 4, 8, 512)] * 3
        body = functools.partial(fine_down_kernel, first)
        if first:
            rhs0, field0, low, edge, cond0, inv0 = call(body, outs + state, scratch, *args, name="fine_down_first")
        else:
            cond0, inv0 = kept[0:2]
            rhs0, field0, low, edge = call(body, outs, scratch, *args, inv0, name="fine_down")
        rows = lax.all_to_all(low, "gy", split_axis=0, concat_axis=0, tiled=True)
        (rows,) = call(pick_kernel, [f32(5, parts, 2, 2, 4, 256)], [], prm, rows, name="pick")
        chip = cores(rows)
        far = cores(pick(across(chip), core))
        near_rows = 192 + (64 if first else 0) + 48 * parts
        outs = [f32(12, 2, 24, 256), f32(8, 2, 24, 256), f32(parts, 2, 24, 128), f32(near_rows, 128)]
        state = [f32(12, 2, 24, 256)] * 2
        scratch = [(12, 2, 24, 256)] * 3
        body = functools.partial(middle_down_kernel, first)
        if first:
            rhs1, field1, low, near, cond1, inv1 = call(
                body, outs + state, scratch, prm, chip, far, name="middle_down_first"
            )
        else:
            cond1, inv1 = kept[2:4]
            rhs1, field1, low, near = call(body, outs, scratch, prm, chip, far, inv1, name="middle_down")
        flat = low.reshape(48 * parts, 128)
        beside = [swap(near, 1), swap(flat, 3), swap(flat, 5)]
        far = cores(jnp.concatenate([edge, *beside], axis=0))
        outs = [f32(4, 4, 4, 512)] * 2
        scratch = [(14, 1, 24, 128)] * 4 + [(14, 2, 16, 256)] + [(12, 2, 16, 256)] * 3 + [(12, 4, 8, 512)] * 3
        args = [prm, low, far, field1, rhs1, cond1, inv1, field0, rhs0, cond0, inv0]
        body = functools.partial(up_kernel, first)
        if first:
            state = [f32(14, 2, 16, 256), f32(14, 1, 24, 128), f32(14, 1, 24, 128)]
            adjoint, remain, *coarse = call(body, outs + state, scratch, *args, name="up_first")
            kept = (cond0, inv0, cond1, inv1, *coarse)
        else:
            adjoint, remain = call(body, outs, scratch, *args, *kept[4:7], adjoint, name="up")
    return tuple(
        call(
            finish_kernel,
            [f32(4, 16, 512)] * 2,
            [(4, 128, 128)],
            adjoint,
            remain,
            scalars=False,
            name="finish",
        )
    )


def solution(mesh):
    placed = (P("gz", "gy", None), P("gz", "gy", None))
    return jax.shard_map(local, mesh=mesh, in_specs=placed, out_specs=placed, check_vma=False)
```
